32 devices in a mesh: groups: 2 (over y), dp: 4 (over z), tensor: 2 (over x), seq: 2 (over core).
Axes of the slice: x: 2, y: 2, z: 4, core: 2. Of those that a mesh axis runs over, the one named last changes fastest.
Arguments:
- inputs: bfloat16 [8192, 4096], P(('groups', 'dp', 'seq'), 'tensor'), parts along dimension 0, may hold values from -6 to 6
- cotangent: bfloat16 [8192, 4096], P(('groups', 'dp', 'seq'), 'tensor'), parts along dimension 0, may hold values from -6 to 6
- gate_pre: bfloat16 [8192, 11008], P(('groups', 'dp', 'seq'), 'tensor'), parts along dimension 0, may hold values from -8 to 8
- down_weight: bfloat16 [11008, 4096], P('tensor', 'dp'), may hold values from -0.0546875 to 0.0546875
- proj_in: bfloat16 [4096, 32], P('tensor'), may hold values from -0.09375 to 0.09375
- proj_out: bfloat16 [11008, 32], P('tensor'), may hold values from -0.0546875 to 0.0546875
- doc_lens: int32 [8, 16], P(('groups', 'dp')), parts along dimension 0, may hold values from 1 to 256, 1024 in all within a row
- queries: float32 [512, 1024], replicated, may hold values from -0.06 to 0.06
Outputs:
- doc_grads: float32 [128, 1024], P(('groups', 'dp')), parts along dimension 0
- fisher: float32 [2048, 1024], P(('groups', 'tensor', 'seq')), parts along dimension 0
- scores: float32 [512, 128], P(None, ('groups', 'dp')), parts along dimension 1
The draws below stay inside these ranges and needn't reach their ends.
There are 2 independent parts, one for each index of `groups`. The reference program is written for one: setup_inputs(seed, part) draws one part's arguments, and reference() takes and returns one part's arrays. A program takes and returns all parts, laid end to end along the dimension named above; an argument that names none is the same for every part. Nothing has to cross between parts.
Inputs may be any that keep to these rules, and one draw needn't show every extreme that they name: `doc_lens`: each row sums to 1024 and its largest entry is exactly 256.
All inputs are finite; a program needn't handle non-finite values.
Results may differ from the reference program's by a relative error of at most 0.0041.
Values may be sent and summed in bfloat16 or wider, within the bound.
No kernel may reach another device: no remote copies, remote signals or barrier semaphores. Data moves between devices by JAX's collectives and lax.ppermute only.
A program may use at most 192 MiB of HBM per device.

```python
import math
import jax
import jax.numpy as jnp
import numpy as np
from jax import lax

D = 4096
FF = 11008
RANK = 32
DOCS = 16
NQ = 512
K = 1024
LEN = 1024
MOST = 256
TOKENS = 4096
DOCS_ALL = 64
N_DP = 4


def steps_of(key, shape, split, low, top_value):
    def one(dim, blocks):
        heights = jax.random.uniform(jax.random.fold_in(jax.random.fold_in(key, 6), dim), (blocks,), jnp.float32, low / len(split), top_value / len(split))
        return jnp.repeat(jnp.exp(heights), shape[dim] // blocks).reshape((-1,) + (1,) * (len(shape) - dim - 1))

    factor_of = one(*split[0])
    for cut in split[1:]:
        factor_of = factor_of * one(*cut)
    return factor_of


def length_profile(amount, total, limit, skew):
    weights = [(1 << 20) // math.isqrt(grade ** skew) + 1 for grade in range(2, amount + 1)]
    spare, holding = total - limit - (amount - 1), [1] * (amount - 1)
    while spare > 0:
        candidates = [i for i in range(amount - 1) if holding[i] < limit]
        mass, budget = sum([weights[i] for i in candidates]), spare
        for i in candidates:
            extra = min(limit - holding[i], max(1, budget * weights[i] // mass), spare)
            holding[i] = holding[i] + extra
            spare = spare - extra
    return np.array([limit] + holding)


def uneven(stream_key, number_of, total, most, skew):
    if number_of == 2:
        one = jax.random.randint(stream_key, (), max(1, total - most), min(most, total - 1) + 1)
        return jnp.stack([one, total - one])
    tallies = jnp.asarray(length_profile(number_of, total, most, skew), jnp.int32)
    couples = (number_of - 1) // 2
    source_of, taker = tallies[1:1 + 2 * couples:2], tallies[2:2 + 2 * couples:2]
    room = jnp.minimum(source_of - 1, most - taker)
    passed = jax.random.randint(jax.random.fold_in(stream_key, 1), (couples,), 0, 1 << 20) % (room + 1)
    tallies = tallies.at[1:1 + 2 * couples:2].set(source_of - passed).at[2:2 + 2 * couples:2].set(taker + passed)
    return tallies[jax.random.permutation(jax.random.fold_in(stream_key, 2), number_of)]


def scatter_about(rng, extent, width, reach, split=(), kind=jnp.bfloat16):
    drawn = width * jax.random.normal(rng, extent, jnp.float32)
    if split:
        drawn = drawn * steps_of(rng, extent, split, -0.22, 0.18)
    return jnp.clip(drawn, -reach, reach).astype(kind)


def setup_inputs(seed: int = 0, part: int = 0) -> dict:
    streams_of = jax.random.split(jax.random.key(seed), 9)
    part_keys = jax.random.split(jax.random.fold_in(streams_of[8], part), 9)
    return {
        "inputs": scatter_about(part_keys[0], (TOKENS, D), 1.0, 6.0, ((0, 8), (1, 2))),
        "cotangent": scatter_about(part_keys[1], (TOKENS, D), 1.0, 6.0, ((0, 8), (1, 2))),
        "gate_pre": scatter_about(part_keys[2], (TOKENS, FF), 1.5, 8.0, ((0, 8), (1, 2))),
        "down_weight": scatter_about(streams_of[3], (FF, D), FF ** -0.5, 0.0546875, ((0, 2), (1, 4))),
        "proj_in": scatter_about(streams_of[4], (D, RANK), D ** -0.5, 0.09375, ((0, 2),)),
        "proj_out": scatter_about(streams_of[5], (FF, RANK), FF ** -0.5, 0.0546875, ((0, 2),)),
        "doc_lens": jax.vmap(lambda own: uneven(own, DOCS, LEN, MOST, 2))(jax.random.split(part_keys[6], N_DP)).reshape((N_DP, DOCS)).astype(jnp.int32),
        "queries": scatter_about(streams_of[7], (NQ, K), 0.01, 0.06, (), jnp.float32),
    }


def one_sequence(packed):
    inputs, cotangent, gate_pre, lens, down_weight, proj_in, proj_out = packed
    hidden_grad = jnp.dot(cotangent.astype(jnp.float32), down_weight.T.astype(jnp.float32), preferred_element_type=jnp.float32)
    up_grad = (hidden_grad * jax.nn.silu(gate_pre.astype(jnp.float32))).astype(jnp.bfloat16)
    left = jnp.dot(up_grad.astype(jnp.float32), proj_out.astype(jnp.float32), preferred_element_type=jnp.float32)
    right = jnp.dot(inputs.astype(jnp.float32), proj_in.astype(jnp.float32), preferred_element_type=jnp.float32)
    ends = jnp.cumsum(lens)
    position = jnp.arange(LEN, dtype=jnp.int32)
    document = jnp.sum((position[:, None] >= ends[None, :]).astype(jnp.int32), axis=1)
    onehot = (document[:, None] == jnp.arange(DOCS, dtype=jnp.int32)[None, :]).astype(jnp.float32)
    grads = jnp.einsum('tc,ti,tj->cij', onehot, left, right, precision=lax.Precision.HIGHEST)
    return grads.reshape(DOCS, K)

def reference(inputs, cotangent, gate_pre, down_weight, proj_in, proj_out, doc_lens, queries):

    def step(index):
        start = index * LEN
        return one_sequence((lax.dynamic_slice_in_dim(inputs, start, LEN, 0), lax.dynamic_slice_in_dim(cotangent, start, LEN, 0), lax.dynamic_slice_in_dim(gate_pre, start, LEN, 0), doc_lens[index], down_weight, proj_in, proj_out))
    doc_grads = lax.map(step, jnp.arange(N_DP, dtype=jnp.int32)).reshape(DOCS_ALL, K)
    raw = jnp.dot(doc_grads.T, doc_grads, precision=lax.Precision.HIGHEST)
    mean_diag = jnp.trace(raw) / K
    fisher = raw / mean_diag
    damped = fisher + jnp.eye(K, dtype=jnp.float32)
    factor = jnp.linalg.cholesky(damped)
    solved = jax.scipy.linalg.cho_solve((factor, True), doc_grads.T)
    scores = jnp.dot(queries, solved, precision=lax.Precision.HIGHEST)
    return (doc_grads, fisher, scores)
```

```python
import jax
import jax.numpy as jnp
from jax import lax
from jax.sharding import PartitionSpec as P

HIGHEST = lax.Precision.HIGHEST
LANES = 128
CHUNKS = 4


def shifted(x, axes, sizes, shift):
    pairs = []
    if isinstance(axes, str):
        (n,) = sizes
        pairs = [(i, (i + shift[0]) % n) for i in range(n)]
    else:
        a, b = sizes
        for i in range(a):
            for j in range(b):
                pairs.append((i * b + j, ((i + shift[0]) % a) * b + (j + shift[1]) % b))
    return lax.ppermute(x, axes, pairs)


def gather_in_order(x, axis, dim):
    n = lax.axis_size(axis)
    me = lax.axis_index(axis)
    shape = list(x.shape)
    shape[dim] *= n
    out = jnp.zeros(shape, x.dtype)
    for r in range(n):
        piece = x if r == 0 else shifted(x, axis, (n,), (r,))
        out = lax.dynamic_update_slice_in_dim(out, piece, ((me - r) % n) * x.shape[dim], dim)
    return out


def sum_over(x, axis):
    n = lax.axis_size(axis)
    if n == 2:
        return x + shifted(x, axis, (2,), (1,))
    return jnp.sum(gather_in_order(x[None], axis, 0), axis=0)


def on_device(inputs, cotangent, gate_pre, down_weight, proj_in, proj_out, doc_lens, queries):
    n_groups, n_seq = lax.axis_size("groups"), lax.axis_size("seq")
    n_dp, n_tensor = lax.axis_size("dp"), lax.axis_size("tensor")
    group, half = lax.axis_index("groups"), lax.axis_index("seq")
    stage, side = lax.axis_index("dp"), lax.axis_index("tensor")
    rows = inputs.shape[0]
    units = gate_pre.shape[1]
    docs = doc_lens.shape[1]
    rank = proj_in.shape[1]
    width = rank * rank
    sharers = n_groups * n_seq
    part = min(units, -(-units // (sharers * LANES)) * LANES)
    pair = ("groups", "seq")
    sizes = (n_groups, n_seq)

    def first_unit(who):
        return jnp.minimum(who * part, units - part)

    mine = group * n_seq + half
    start = first_unit(mine)
    tiles = -(-part // LANES)
    bounds = sorted({min(part, -(-tiles * c // CHUNKS) * LANES) for c in range(CHUNKS + 1)})

    gathered = []
    token = None
    for low, high in zip(bounds[:-1], bounds[1:]):
        block = lax.dynamic_slice_in_dim(down_weight, start + low, high - low, 0)
        gathered.append(lax.all_gather(block, "dp", axis=1, tiled=True))

    order = [(dg, ds) for dg in range(n_groups) for ds in range(n_seq)]
    cots = []
    for dg in range(n_groups):
        own = cotangent if dg == 0 else shifted(cotangent, "groups", (n_groups,), (dg,))
        full = gather_in_order(own, "tensor", 1)
        for ds in range(n_seq):
            cots.append(full if ds == 0 else shifted(full, "seq", (n_seq,), (ds,)))
    gates = []
    for dg, ds in order:
        to = ((group + dg) % n_groups) * n_seq + (half + ds) % n_seq
        columns = lax.dynamic_slice_in_dim(gate_pre, first_unit(to), part, 1)
        gates.append(columns if dg == ds == 0 else shifted(columns, pair, sizes, (dg, ds)))

    right = sum_over(jnp.dot(inputs, proj_in, preferred_element_type=jnp.float32), "tensor")
    rights = [right if dg == ds == 0 else shifted(right, pair, sizes, (dg, ds)) for dg, ds in order]
    lens = [doc_lens if dg == 0 else shifted(doc_lens, "groups", (n_groups,), (dg,)) for dg in range(n_groups)]

    cot = jnp.concatenate(cots, axis=0)
    gate = jnp.concatenate(gates, axis=0)
    slope = jax.nn.silu(gate.astype(jnp.float32))
    numbers = start + jnp.arange(part, dtype=jnp.int32)
    out_factor = lax.dynamic_slice_in_dim(proj_out, start, part, 0)
    out_factor = jnp.where((numbers >= mine * part)[:, None], out_factor, 0).astype(proj_out.dtype)

    left = 0.0
    for weight, low, high in zip(gathered, bounds[:-1], bounds[1:]):
        hidden_grad = lax.dot_general(
            cot, weight, (((1,), (1,)), ((), ())), preferred_element_type=jnp.float32
        )
        up_grad = (hidden_grad * slope[:, low:high]).astype(jnp.bfloat16)
        left = left + jnp.dot(up_grad, out_factor[low:high], preferred_element_type=jnp.float32)

    parts = []
    for dg in range(n_groups):
        ends = jnp.cumsum(lens[dg][0])
        position = jnp.concatenate(
            [((half - ds) % n_seq) * rows + jnp.arange(rows, dtype=jnp.int32) for ds in range(n_seq)]
        )
        document = jnp.sum((position[:, None] >= ends[None, :]).astype(jnp.int32), axis=1)
        onehot = (document[:, None] == jnp.arange(docs, dtype=jnp.int32)[None, :]).astype(jnp.float32)
        span = slice(dg * n_seq * rows, (dg + 1) * n_seq * rows)
        right_block = jnp.concatenate(rights[dg * n_seq:(dg + 1) * n_seq], axis=0)
        grads = jnp.einsum(
            "tc,ti,tj->cij", onehot, left[span], right_block, precision=HIGHEST
        ).reshape(docs, width)
        parts.append(grads)
    grads = parts[0]
    if n_groups == 2:
        grads = grads + shifted(parts[1], "groups", (2,), (1,))
    else:
        for dg in range(1, n_groups):
            grads = grads + shifted(parts[dg], "groups", (n_groups,), (-dg,))
    doc_grads = sum_over(sum_over(grads, "tensor"), "seq")

    every = gather_in_order(doc_grads, "dp", 0)
    mean_diag = jnp.sum(every * every) / width
    pieces = n_tensor * n_seq
    share = width // pieces
    which = side * n_seq + half
    columns = lax.dynamic_slice_in_dim(every, which * share, share, 1)
    fisher_rows = lax.dot_general(
        columns, every, (((0,), (0,)), ((), ())), precision=HIGHEST, preferred_element_type=jnp.float32
    ) / mean_diag

    total = every.shape[0]
    gram = lax.dot_general(
        every, every, (((1,), (1,)), ((), ())), precision=HIGHEST, preferred_element_type=jnp.float32
    )
    damped = gram / mean_diag + jnp.eye(total, dtype=jnp.float32)
    factor = jnp.linalg.cholesky(damped)
    chosen = (jnp.arange(total)[:, None] == stage * docs + jnp.arange(docs)[None, :]).astype(jnp.float32)
    solved = jax.scipy.linalg.cho_solve((factor, True), chosen)
    products = lax.dot_general(
        queries, every, (((1,), (1,)), ((), ())), precision=HIGHEST, preferred_element_type=jnp.float32
    )
    scores = jnp.dot(products, solved, precision=HIGHEST)
    return (doc_grads, fisher_rows, scores)


def solution(mesh):
    return jax.shard_map(
        on_device,
        mesh=mesh,
        in_specs=(
            P(("groups", "dp", "seq"), "tensor"),
            P(("groups", "dp", "seq"), "tensor"),
            P(("groups", "dp", "seq"), "tensor"),
            P("tensor", "dp"),
            P("tensor", None),
            P("tensor", None),
            P(("groups", "dp"), None),
            P(),
        ),
        out_specs=(
            P(("groups", "dp"), None),
            P(("groups", "tensor", "seq"), None),
            P(None, ("groups", "dp")),
        ),
        check_vma=False,
    )
```

```python
import functools

import jax
import jax.numpy as jnp
from jax import lax
from jax.experimental import pallas as pl
from jax.experimental.pallas import tpu as pltpu
from jax.sharding import PartitionSpec as P

HIGHEST = lax.Precision.HIGHEST
CHUNK = 384


def shifted(x, axes, sizes, shift):
    if isinstance(axes, str):
        (n,) = sizes
        pairs = [(i, (i + shift[0]) % n) for i in range(n)]
    else:
        a, b = sizes
        pairs = [
            (i * b + j, ((i + shift[0]) % a) * b + (j + shift[1]) % b)
            for i in range(a) for j in range(b)
        ]
    return lax.ppermute(x, axes, pairs)


def in_order(pieces, axis, dim):
    n = len(pieces)
    me = lax.axis_index(axis)
    shape = list(pieces[0].shape)
    size = shape[dim]
    shape[dim] *= n
    out = jnp.zeros(shape, pieces[0].dtype)
    for r, piece in enumerate(pieces):
        out = lax.dynamic_update_slice_in_dim(out, piece, ((me - r) % n) * size, dim)
    return out


def gather_in_order(x, axis, dim):
    n = lax.axis_size(axis)
    return in_order([x if r == 0 else shifted(x, axis, (n,), (r,)) for r in range(n)], axis, dim)


def sum_over(x, axis):
    n = lax.axis_size(axis)
    if n == 2:
        return x + shifted(x, axis, (2,), (1,))
    return jnp.sum(gather_in_order(x[None], axis, 0), axis=0)


def chunk_kernel(n, me_ref, cot_ref, gate_ref, factor_ref, before_ref, *rest):
    slots, (after_ref, weight, sems) = rest[:n], rest[n:]
    columns = slots[0].shape[1]

    @pl.when(pl.program_id(0) == 0)
    def _():
        copies = []
        for r in range(n):
            at = pl.multiple_of(lax.rem(me_ref[0] + (n - r), n) * columns, columns)
            copies.append(pltpu.make_async_copy(slots[r], weight.at[:, pl.ds(at, columns)], sems.at[r]))
        for copy in copies:
            copy.start()
        for copy in copies:
            copy.wait()

    hidden = lax.dot_general(
        cot_ref[...], weight[...], (((1,), (1,)), ((), ())), preferred_element_type=jnp.float32
    )
    gate = gate_ref[...].astype(jnp.float32)
    up_grad = (hidden * (gate / (1.0 + jnp.exp(-gate)))).astype(jnp.bfloat16)
    after_ref[...] = before_ref[...] + jnp.dot(
        up_grad, factor_ref[...], preferred_element_type=jnp.float32
    )


def add_chunk(me, cot, gate, factor, before, slots, tile):
    tokens, depth = cot.shape
    height = gate.shape[1]
    rank = factor.shape[1]
    n = len(slots)
    return pl.pallas_call(
        functools.partial(chunk_kernel, n),
        out_shape=jax.ShapeDtypeStruct((tokens, rank), jnp.float32),
        grid_spec=pltpu.PrefetchScalarGridSpec(
            num_scalar_prefetch=1,
            grid=(tokens // tile,),
            in_specs=[
                pl.BlockSpec((tile, depth), lambda i, me: (i, 0)),
                pl.BlockSpec((tile, height), lambda i, me: (i, 0)),
                pl.BlockSpec((height, rank), lambda i, me: (0, 0)),
                pl.BlockSpec((tile, rank), lambda i, me: (i, 0)),
            ] + [pl.BlockSpec(memory_space=pl.ANY)] * n,
            out_specs=pl.BlockSpec((tile, rank), lambda i, me: (i, 0)),
            scratch_shapes=[
                pltpu.VMEM((height, depth), jnp.bfloat16),
                pltpu.SemaphoreType.DMA((n,)),
            ],
        ),
        compiler_params=pltpu.CompilerParams(vmem_limit_bytes=40 * 1024 * 1024),
        cost_estimate=pl.CostEstimate(
            flops=2 * tokens * depth * height,
            bytes_accessed=2 * (tokens * depth + height * depth + tokens * height),
            transcendentals=tokens * height,
        ),
    )(me, cot, gate, factor, before, *slots)


def on_device(inputs, cotangent, gate_pre, down_weight, proj_in, proj_out, doc_lens, queries):
    n_groups, n_seq = lax.axis_size("groups"), lax.axis_size("seq")
    n_dp, n_tensor = lax.axis_size("dp"), lax.axis_size("tensor")
    group, half = lax.axis_index("groups"), lax.axis_index("seq")
    stage, side = lax.axis_index("dp"), lax.axis_index("tensor")
    rows = inputs.shape[0]
    units = gate_pre.shape[1]
    docs = doc_lens.shape[1]
    rank = proj_in.shape[1]
    width = rank * rank
    part = units // (n_groups * n_seq)
    pair = ("groups", "seq")
    sizes = (n_groups, n_seq)
    mine = group * n_seq + half

    bounds = list(range(0, part, CHUNK)) + [part]
    spans = list(zip(bounds[:-1], bounds[1:]))
    chunks = [
        [lax.dynamic_slice_in_dim(down_weight, mine * part + low, high - low, 0)] for low, high in spans
    ]
    sent = []
    for first in range(0, len(chunks), 2):
        for _ in range(n_dp - 1):
            for slots in chunks[first:first + 2]:
                block = slots[-1]
                if len(sent) >= 2:
                    block, sent[-2][-1] = lax.optimization_barrier((block, sent[-2][-1]))
                slots.append(shifted(block, "dp", (n_dp,), (1,)))
                sent.append(slots)

    order = [(dg, ds) for dg in range(n_groups) for ds in range(n_seq)]
    cots = []
    for dg in range(n_groups):
        own = cotangent if dg == 0 else shifted(cotangent, "groups", (n_groups,), (dg,))
        pieces = [own if r == 0 else shifted(own, "tensor", (n_tensor,), (r,)) for r in range(n_tensor)]
        for ds in range(n_seq):
            cots.append(in_order(
                pieces if ds == 0 else [shifted(x, "seq", (n_seq,), (ds,)) for x in pieces], "tensor", 1
            ))
    gates = []
    for dg, ds in order:
        to = ((group + dg) % n_groups) * n_seq + (half + ds) % n_seq
        columns = lax.dynamic_slice_in_dim(gate_pre, to * part, part, 1)
        gates.append(columns if dg == ds == 0 else shifted(columns, pair, sizes, (dg, ds)))

    right = sum_over(jnp.dot(inputs, proj_in, preferred_element_type=jnp.float32), "tensor")
    rights = [right if dg == ds == 0 else shifted(right, pair, sizes, (dg, ds)) for dg, ds in order]
    lens = [doc_lens if dg == 0 else shifted(doc_lens, "groups", (n_groups,), (dg,)) for dg in range(n_groups)]

    cot = jnp.concatenate(cots, axis=0)
    gate = jnp.concatenate(gates, axis=0)
    out_factor = lax.dynamic_slice_in_dim(proj_out, mine * part, part, 0)
    me = jnp.reshape(stage, (1,)).astype(jnp.int32)

    left = jnp.zeros((n_groups * n_seq * rows, rank), jnp.float32)
    for slots, (low, high) in zip(chunks, spans):
        left = add_chunk(me, cot, gate[:, low:high], out_factor[low:high], left, slots, rows)

    parts = []
    for dg in range(n_groups):
        ends = jnp.cumsum(lens[dg][0])
        position = jnp.concatenate(
            [((half - ds) % n_seq) * rows + jnp.arange(rows, dtype=jnp.int32) for ds in range(n_seq)]
        )
        document = jnp.sum((position[:, None] >= ends[None, :]).astype(jnp.int32), axis=1)
        onehot = (document[:, None] == jnp.arange(docs, dtype=jnp.int32)[None, :]).astype(jnp.float32)
        span = slice(dg * n_seq * rows, (dg + 1) * n_seq * rows)
        right_block = jnp.concatenate(rights[dg * n_seq:(dg + 1) * n_seq], axis=0)
        grads = jnp.einsum(
            "tc,ti,tj->cij", onehot, left[span], right_block, precision=HIGHEST
        ).reshape(docs, width)
        parts.append(grads)
    grads = parts[0]
    for dg in range(1, n_groups):
        grads = grads + shifted(parts[dg], "groups", (n_groups,), (-dg,))
    doc_grads = sum_over(sum_over(grads, "tensor"), "seq")

    every = gather_in_order(doc_grads, "dp", 0)
    mean_diag = jnp.sum(every * every) / width
    pieces = n_tensor * n_seq
    share = width // pieces
    which = side * n_seq + half
    columns = lax.dynamic_slice_in_dim(every, which * share, share, 1)
    fisher_rows = lax.dot_general(
        columns, every, (((0,), (0,)), ((), ())), precision=HIGHEST, preferred_element_type=jnp.float32
    ) / mean_diag

    total = every.shape[0]
    gram = lax.dot_general(
        every, every, (((1,), (1,)), ((), ())), precision=HIGHEST, preferred_element_type=jnp.float32
    )
    damped = gram / mean_diag + jnp.eye(total, dtype=jnp.float32)
    factor = jnp.linalg.cholesky(damped)
    chosen = (jnp.arange(total)[:, None] == stage * docs + jnp.arange(docs)[None, :]).astype(jnp.float32)
    solved = jax.scipy.linalg.cho_solve((factor, True), chosen)
    products = lax.dot_general(
        queries, every, (((1,), (1,)), ((), ())), precision=HIGHEST, preferred_element_type=jnp.float32
    )
    scores = jnp.dot(products, solved, precision=HIGHEST)
    return (doc_grads, fisher_rows, scores)


def solution(mesh):
    return jax.shard_map(
        on_device,
        mesh=mesh,
        in_specs=(
            P(("groups", "dp", "seq"), "tensor"),
            P(("groups", "dp", "seq"), "tensor"),
            P(("groups", "dp", "seq"), "tensor"),
            P("tensor", "dp"),
            P("tensor", None),
            P("tensor", None),
            P(("groups", "dp"), None),
            P(),
        ),
        out_specs=(
            P(("groups", "dp"), None),
            P(("groups", "tensor", "seq"), None),
            P(None, ("groups", "dp")),
        ),
        check_vma=False,
    )
```

```python
import functools

import jax
import jax.numpy as jnp
from jax import lax
from jax.experimental import pallas as pl
from jax.experimental.pallas import tpu as pltpu
from jax.sharding import PartitionSpec as P

HIGHEST = lax.Precision.HIGHEST
LAST = 256


def shifted(x, axes, sizes, shift):
    if isinstance(axes, str):
        (n,) = sizes
        pairs = [(i, (i + shift[0]) % n) for i in range(n)]
    else:
        a, b = sizes
        pairs = [
            (i * b + j, ((i + shift[0]) % a) * b + (j + shift[1]) % b)
            for i in range(a) for j in range(b)
        ]
    return lax.ppermute(x, axes, pairs)


def in_order(pieces, axis, dim):
    n = len(pieces)
    me = lax.axis_index(axis)
    shape = list(pieces[0].shape)
    size = shape[dim]
    shape[dim] *= n
    out = jnp.zeros(shape, pieces[0].dtype)
    for r, piece in enumerate(pieces):
        out = lax.dynamic_update_slice_in_dim(out, piece, ((me - r) % n) * size, dim)
    return out


def gather_in_order(x, axis, dim):
    n = lax.axis_size(axis)
    return in_order([x if r == 0 else shifted(x, axis, (n,), (r,)) for r in range(n)], axis, dim)


def sum_over(x, axis):
    n = lax.axis_size(axis)
    if n == 2:
        return x + shifted(x, axis, (2,), (1,))
    return jnp.sum(gather_in_order(x[None], axis, 0), axis=0)


def chunk_kernel(contract, cot_ref, gate_ref, factor_ref, before_ref, weight_ref, after_ref):
    hidden = lax.dot_general(
        cot_ref[...], weight_ref[...], (((1,), (contract,)), ((), ())), preferred_element_type=jnp.float32
    )
    gate = gate_ref[...].astype(jnp.float32)
    up_grad = (hidden * (gate / (1.0 + jnp.exp(-gate)))).astype(jnp.bfloat16)
    after_ref[...] = before_ref[...] + jnp.dot(
        up_grad, factor_ref[...], preferred_element_type=jnp.float32
    )


def add_chunk(cot, gate, factor, before, weight, contract, tile):
    tokens, depth = cot.shape
    height = gate.shape[1]
    rank = factor.shape[1]
    return pl.pallas_call(
        functools.partial(chunk_kernel, contract),
        out_shape=jax.ShapeDtypeStruct((tokens, rank), jnp.float32),
        grid=(tokens // tile,),
        in_specs=[
            pl.BlockSpec((tile, depth), lambda i: (i, 0)),
            pl.BlockSpec((tile, height), lambda i: (i, 0)),
            pl.BlockSpec((height, rank), lambda i: (0, 0)),
            pl.BlockSpec((tile, rank), lambda i: (i, 0)),
            pl.BlockSpec(weight.shape, lambda i: (0, 0)),
        ],
        out_specs=pl.BlockSpec((tile, rank), lambda i: (i, 0)),
        compiler_params=pltpu.CompilerParams(vmem_limit_bytes=44 * 1024 * 1024),
        cost_estimate=pl.CostEstimate(
            flops=2 * tokens * depth * height,
            bytes_accessed=2 * (tokens * depth + height * depth + tokens * height),
            transcendentals=tokens * height,
        ),
    )(cot, gate, factor, before, weight)


def on_device(inputs, cotangent, gate_pre, down_weight, proj_in, proj_out, doc_lens, queries):
    n_groups, n_seq = lax.axis_size("groups"), lax.axis_size("seq")
    n_dp, n_tensor = lax.axis_size("dp"), lax.axis_size("tensor")
    group, half = lax.axis_index("groups"), lax.axis_index("seq")
    stage, side = lax.axis_index("dp"), lax.axis_index("tensor")
    rows = inputs.shape[0]
    units = gate_pre.shape[1]
    docs = doc_lens.shape[1]
    rank = proj_in.shape[1]
    width = rank * rank
    part = units // (n_groups * n_seq)
    pair = ("groups", "seq")
    sizes = (n_groups, n_seq)
    mine = group * n_seq + half

    early = lax.all_gather(
        lax.dynamic_slice_in_dim(down_weight, mine * part + LAST, part - LAST, 0), "dp", axis=1, tiled=True
    )
    piece = lax.dynamic_slice_in_dim(down_weight, mine * part, LAST, 0).T
    piece, early = lax.optimization_barrier((piece, early))
    late = lax.all_gather(piece, "dp", axis=0, tiled=True)

    order = [(dg, ds) for dg in range(n_groups) for ds in range(n_seq)]
    cots = []
    for dg in range(n_groups):
        own = cotangent if dg == 0 else shifted(cotangent, "groups", (n_groups,), (dg,))
        pieces = [own if r == 0 else shifted(own, "tensor", (n_tensor,), (r,)) for r in range(n_tensor)]
        for ds in range(n_seq):
            cots.append(in_order(
                pieces if ds == 0 else [shifted(x, "seq", (n_seq,), (ds,)) for x in pieces], "tensor", 1
            ))
    gates = []
    for dg, ds in order:
        to = ((group + dg) % n_groups) * n_seq + (half + ds) % n_seq
        columns = lax.dynamic_slice_in_dim(gate_pre, to * part, part, 1)
        gates.append(columns if dg == ds == 0 else shifted(columns, pair, sizes, (dg, ds)))

    cot = jnp.concatenate(cots, axis=0)
    gate = jnp.concatenate(gates, axis=0)
    right_part = jnp.dot(inputs, proj_in, preferred_element_type=jnp.float32)
    right_part, doc_lens, cot, gate = lax.optimization_barrier((right_part, doc_lens, cot, gate))
    right = sum_over(right_part, "tensor")
    rights = [right if dg == ds == 0 else shifted(right, pair, sizes, (dg, ds)) for dg, ds in order]
    lens = [doc_lens if dg == 0 else shifted(doc_lens, "groups", (n_groups,), (dg,)) for dg in range(n_groups)]

    out_factor = lax.dynamic_slice_in_dim(proj_out, mine * part, part, 0)
    left = jnp.zeros((n_groups * n_seq * rows, rank), jnp.float32)
    left = add_chunk(cot, gate[:, LAST:], out_factor[LAST:], left, early, 1, rows)
    left = add_chunk(cot, gate[:, :LAST], out_factor[:LAST], left, late, 0, rows)

    parts = []
    for dg in range(n_groups):
        ends = jnp.cumsum(lens[dg][0])
        position = jnp.concatenate(
            [((half - ds) % n_seq) * rows + jnp.arange(rows, dtype=jnp.int32) for ds in range(n_seq)]
        )
        document = jnp.sum((position[:, None] >= ends[None, :]).astype(jnp.int32), axis=1)
        onehot = (document[:, None] == jnp.arange(docs, dtype=jnp.int32)[None, :]).astype(jnp.float32)
        span = slice(dg * n_seq * rows, (dg + 1) * n_seq * rows)
        right_block = jnp.concatenate(rights[dg * n_seq:(dg + 1) * n_seq], axis=0)
        grads = jnp.einsum(
            "tc,ti,tj->cij", onehot, left[span], right_block, precision=HIGHEST
        ).reshape(docs, width)
        parts.append(grads)
    grads = parts[0]
    for dg in range(1, n_groups):
        grads = grads + shifted(parts[dg], "groups", (n_groups,), (-dg,))
    doc_grads = sum_over(sum_over(grads, "tensor"), "seq")

    every = gather_in_order(doc_grads, "dp", 0)
    mean_diag = jnp.sum(every * every) / width
    pieces = n_tensor * n_seq
    share = width // pieces
    which = side * n_seq + half
    columns = lax.dynamic_slice_in_dim(every, which * share, share, 1)
    fisher_rows = lax.dot_general(
        columns, every, (((0,), (0,)), ((), ())), precision=HIGHEST, preferred_element_type=jnp.float32
    ) / mean_diag

    total = every.shape[0]
    gram = lax.dot_general(
        every, every, (((1,), (1,)), ((), ())), precision=HIGHEST, preferred_element_type=jnp.float32
    )
    damped = gram / mean_diag + jnp.eye(total, dtype=jnp.float32)
    factor = jnp.linalg.cholesky(damped)
    chosen = (jnp.arange(total)[:, None] == stage * docs + jnp.arange(docs)[None, :]).astype(jnp.float32)
    solved = jax.scipy.linalg.cho_solve((factor, True), chosen)
    products = lax.dot_general(
        queries, every, (((1,), (1,)), ((), ())), precision=HIGHEST, preferred_element_type=jnp.float32
    )
    scores = jnp.dot(products, solved, precision=HIGHEST)
    return (doc_grads, fisher_rows, scores)


def solution(mesh):
    return jax.shard_map(
        on_device,
        mesh=mesh,
        in_specs=(
            P(("groups", "dp", "seq"), "tensor"),
            P(("groups", "dp", "seq"), "tensor"),
            P(("groups", "dp", "seq"), "tensor"),
            P("tensor", "dp"),
            P("tensor", None),
            P("tensor", None),
            P(("groups", "dp"), None),
            P(),
        ),
        out_specs=(
            P(("groups", "dp"), None),
            P(("groups", "tensor", "seq"), None),
            P(None, ("groups", "dp")),
        ),
        check_vma=False,
    )
```

```python
import functools

import jax
import jax.numpy as jnp
from jax import lax
from jax.experimental import pallas as pl
from jax.experimental.pallas import tpu as pltpu
from jax.sharding import PartitionSpec as P

HIGHEST = lax.Precision.HIGHEST
LAST = 256


def shifted(x, axes, sizes, shift):
    if isinstance(axes, str):
        (n,) = sizes
        pairs = [(i, (i + shift[0]) % n) for i in range(n)]
    else:
        a, b = sizes
        pairs = [
            (i * b + j, ((i + shift[0]) % a) * b + (j + shift[1]) % b)
            for i in range(a) for j in range(b)
        ]
    return lax.ppermute(x, axes, pairs)


def in_order(pieces, axis, dim):
    n = len(pieces)
    me = lax.axis_index(axis)
    shape = list(pieces[0].shape)
    size = shape[dim]
    shape[dim] *= n
    out = jnp.zeros(shape, pieces[0].dtype)
    for r, piece in enumerate(pieces):
        out = lax.dynamic_update_slice_in_dim(out, piece, ((me - r) % n) * size, dim)
    return out


def gather_in_order(x, axis, dim):
    n = lax.axis_size(axis)
    return in_order([x if r == 0 else shifted(x, axis, (n,), (r,)) for r in range(n)], axis, dim)


def sum_over(x, axis):
    n = lax.axis_size(axis)
    if n == 2:
        return x + shifted(x, axis, (2,), (1,))
    return jnp.sum(gather_in_order(x[None], axis, 0), axis=0)


def chunk_kernel(n_blocks, n_tensor, contract, skip, side_ref, *refs):
    refs = list(refs)
    cots = [refs[b * n_tensor:(b + 1) * n_tensor] for b in range(n_blocks)]
    gates = refs[n_blocks * n_tensor:n_blocks * (n_tensor + 1)]
    factor_ref, before_ref, weight_ref, after_ref, cot_buf, gate_buf, sems = refs[n_blocks * (n_tensor + 1):]
    rows, columns = cots[0][0].shape
    gate_width = gate_buf.shape[2]

    def copies(b):
        slot = b % 2
        out = []
        for r in range(n_tensor):
            at = pl.multiple_of(lax.rem(side_ref[0] + (n_tensor - r), n_tensor) * columns, columns)
            out.append(pltpu.make_async_copy(
                cots[b][r], cot_buf.at[slot, :, pl.ds(at, columns)], sems.at[slot, r]
            ))
        source = gates[b] if gate_width == gates[b].shape[1] else gates[b].at[:, pl.ds(0, gate_width)]
        out.append(pltpu.make_async_copy(source, gate_buf.at[slot], sems.at[slot, n_tensor]))
        return out

    for copy in copies(0):
        copy.start()
    for b in range(n_blocks):
        if b + 1 < n_blocks:
            for copy in copies(b + 1):
                copy.start()
        for copy in copies(b):
            copy.wait()
        slot = b % 2
        hidden = lax.dot_general(
            cot_buf[slot], weight_ref[...], (((1,), (contract,)), ((), ())),
            preferred_element_type=jnp.float32,
        )
        gate = gate_buf[slot, :, skip:].astype(jnp.float32)
        up_grad = (hidden * (gate / (1.0 + jnp.exp(-gate)))).astype(jnp.bfloat16)
        after_ref[pl.ds(b * rows, rows), :] = before_ref[pl.ds(b * rows, rows), :] + jnp.dot(
            up_grad, factor_ref[...], preferred_element_type=jnp.float32
        )


def add_chunk(side, cots, gates, skip, factor, before, weight, contract, limit):
    n_blocks, n_tensor = len(cots), len(cots[0])
    rows, columns = cots[0][0].shape
    height, rank = factor.shape
    tokens, depth = n_blocks * rows, n_tensor * columns
    width = gates[0].shape[1] if skip else height
    in_vmem = pl.BlockSpec(memory_space=pltpu.VMEM)
    return pl.pallas_call(
        functools.partial(chunk_kernel, n_blocks, n_tensor, contract, skip),
        out_shape=jax.ShapeDtypeStruct((tokens, rank), jnp.float32),
        in_specs=[pl.BlockSpec(memory_space=pltpu.SMEM)]
        + [pl.BlockSpec(memory_space=pl.ANY)] * (n_blocks * (n_tensor + 1)) + [in_vmem] * 3,
        out_specs=in_vmem,
        scratch_shapes=[
            pltpu.VMEM((2, rows, depth), jnp.bfloat16),
            pltpu.VMEM((2, rows, width), jnp.bfloat16),
            pltpu.SemaphoreType.DMA((2, n_tensor + 1)),
        ],
        compiler_params=pltpu.CompilerParams(vmem_limit_bytes=limit * 1024 * 1024),
        cost_estimate=pl.CostEstimate(
            flops=2 * tokens * depth * height,
            bytes_accessed=2 * (tokens * depth + height * depth + tokens * height),
            transcendentals=tokens * height,
        ),
    )(side, *[piece for pieces in cots for piece in pieces], *gates, factor, before, weight)


def on_device(inputs, cotangent, gate_pre, down_weight, proj_in, proj_out, doc_lens, queries):
    n_groups, n_seq = lax.axis_size("groups"), lax.axis_size("seq")
    n_dp, n_tensor = lax.axis_size("dp"), lax.axis_size("tensor")
    group, half = lax.axis_index("groups"), lax.axis_index("seq")
    stage, side = lax.axis_index("dp"), lax.axis_index("tensor")
    rows = inputs.shape[0]
    units = gate_pre.shape[1]
    docs = doc_lens.shape[1]
    rank = proj_in.shape[1]
    width = rank * rank
    part = units // (n_groups * n_seq)
    pair = ("groups", "seq")
    sizes = (n_groups, n_seq)
    mine = group * n_seq + half

    early = lax.all_gather(
        lax.dynamic_slice_in_dim(down_weight, mine * part + LAST, part - LAST, 0), "dp", axis=1, tiled=True
    )
    piece = lax.dynamic_slice_in_dim(down_weight, mine * part, LAST, 0).T
    piece, early = lax.optimization_barrier((piece, early))
    late = lax.all_gather(piece, "dp", axis=0, tiled=True)

    order = [(dg, ds) for dg in range(n_groups) for ds in range(n_seq)]
    cots = []
    for dg in range(n_groups):
        own = cotangent if dg == 0 else shifted(cotangent, "groups", (n_groups,), (dg,))
        pieces = [own if r == 0 else shifted(own, "tensor", (n_tensor,), (r,)) for r in range(n_tensor)]
        for ds in range(n_seq):
            cots.append(pieces if ds == 0 else [shifted(x, "seq", (n_seq,), (ds,)) for x in pieces])
    gates = []
    for dg, ds in order:
        to = ((group + dg) % n_groups) * n_seq + (half + ds) % n_seq
        columns = lax.dynamic_slice_in_dim(gate_pre, to * part, part, 1)
        gates.append(columns if dg == ds == 0 else shifted(columns, pair, sizes, (dg, ds)))

    right_part = jnp.dot(inputs, proj_in, preferred_element_type=jnp.float32)
    right_part, doc_lens, cots, gates = lax.optimization_barrier((right_part, doc_lens, cots, gates))
    right = sum_over(right_part, "tensor")
    rights = [right if dg == ds == 0 else shifted(right, pair, sizes, (dg, ds)) for dg, ds in order]
    lens = [doc_lens if dg == 0 else shifted(doc_lens, "groups", (n_groups,), (dg,)) for dg in range(n_groups)]

    out_factor = lax.dynamic_slice_in_dim(proj_out, mine * part, part, 0)
    left = jnp.zeros((n_groups * n_seq * rows, rank), jnp.float32)
    where = jnp.reshape(side, (1,)).astype(jnp.int32)
    left = add_chunk(where, cots, gates, LAST, out_factor[LAST:], left, early, 1, 32)
    left = add_chunk(where, cots, gates, 0, out_factor[:LAST], left, late, 0, 18)

    parts = []
    for dg in range(n_groups):
        ends = jnp.cumsum(lens[dg][0])
        position = jnp.concatenate(
            [((half - ds) % n_seq) * rows + jnp.arange(rows, dtype=jnp.int32) for ds in range(n_seq)]
        )
        document = jnp.sum((position[:, None] >= ends[None, :]).astype(jnp.int32), axis=1)
        onehot = (document[:, None] == jnp.arange(docs, dtype=jnp.int32)[None, :]).astype(jnp.float32)
        span = slice(dg * n_seq * rows, (dg + 1) * n_seq * rows)
        right_block = jnp.concatenate(rights[dg * n_seq:(dg + 1) * n_seq], axis=0)
        grads = jnp.einsum(
            "tc,ti,tj->cij", onehot, left[span], right_block, precision=HIGHEST
        ).reshape(docs, width)
        parts.append(grads)
    grads = parts[0]
    for dg in range(1, n_groups):
        grads = grads + shifted(parts[dg], "groups", (n_groups,), (-dg,))
    doc_grads = sum_over(sum_over(grads, "tensor"), "seq")

    every = gather_in_order(doc_grads, "dp", 0)
    mean_diag = jnp.sum(every * every) / width
    pieces = n_tensor * n_seq
    share = width // pieces
    which = side * n_seq + half
    columns = lax.dynamic_slice_in_dim(every, which * share, share, 1)
    fisher_rows = lax.dot_general(
        columns, every, (((0,), (0,)), ((), ())), precision=HIGHEST, preferred_element_type=jnp.float32
    ) / mean_diag

    total = every.shape[0]
    gram = lax.dot_general(
        every, every, (((1,), (1,)), ((), ())), precision=HIGHEST, preferred_element_type=jnp.float32
    )
    damped = gram / mean_diag + jnp.eye(total, dtype=jnp.float32)
    factor = jnp.linalg.cholesky(damped)
    chosen = (jnp.arange(total)[:, None] == stage * docs + jnp.arange(docs)[None, :]).astype(jnp.float32)
    solved = jax.scipy.linalg.cho_solve((factor, True), chosen)
    products = lax.dot_general(
        queries, every, (((1,), (1,)), ((), ())), precision=HIGHEST, preferred_element_type=jnp.float32
    )
    scores = jnp.dot(products, solved, precision=HIGHEST)
    return (doc_grads, fisher_rows, scores)


def solution(mesh):
    return jax.shard_map(
        on_device,
        mesh=mesh,
        in_specs=(
            P(("groups", "dp", "seq"), "tensor"),
            P(("groups", "dp", "seq"), "tensor"),
            P(("groups", "dp", "seq"), "tensor"),
            P("tensor", "dp"),
            P("tensor", None),
            P("tensor", None),
            P(("groups", "dp"), None),
            P(),
        ),
        out_specs=(
            P(("groups", "dp"), None),
            P(("groups", "tensor", "seq"), None),
            P(None, ("groups", "dp")),
        ),
        check_vma=False,
    )
```

```python
import functools

import jax
import jax.numpy as jnp
from jax import lax
from jax.experimental import pallas as pl
from jax.experimental.pallas import tpu as pltpu
from jax.sharding import PartitionSpec as P

HIGHEST = lax.Precision.HIGHEST
LAST = 256
LANES = 128


def shifted(x, axes, sizes, shift):
    if isinstance(axes, str):
        (n,) = sizes
        pairs = [(i, (i + shift[0]) % n) for i in range(n)]
    else:
        a, b = sizes
        pairs = [
            (i * b + j, ((i + shift[0]) % a) * b + (j + shift[1]) % b)
            for i in range(a) for j in range(b)
        ]
    return lax.ppermute(x, axes, pairs)


def in_order(pieces, axis, dim):
    n = len(pieces)
    me = lax.axis_index(axis)
    shape = list(pieces[0].shape)
    size = shape[dim]
    shape[dim] *= n
    out = jnp.zeros(shape, pieces[0].dtype)
    for r, piece in enumerate(pieces):
        out = lax.dynamic_update_slice_in_dim(out, piece, ((me - r) % n) * size, dim)
    return out


def gather_in_order(x, axis, dim):
    n = lax.axis_size(axis)
    return in_order([x if r == 0 else shifted(x, axis, (n,), (r,)) for r in range(n)], axis, dim)


def sum_over(x, axis):
    n = lax.axis_size(axis)
    if n == 2:
        return x + shifted(x, axis, (2,), (1,))
    return jnp.sum(gather_in_order(x[None], axis, 0), axis=0)


def chunk_kernel(contract, cot_ref, gate_ref, factor_ref, before_ref, weight_ref, after_ref):
    hidden = lax.dot_general(
        cot_ref[...], weight_ref[...], (((1,), (contract,)), ((), ())), preferred_element_type=jnp.float32
    )
    gate = gate_ref[...].astype(jnp.float32)
    up_grad = (hidden * (gate / (1.0 + jnp.exp(-gate)))).astype(jnp.bfloat16)
    after_ref[...] = before_ref[...] + jnp.dot(
        up_grad, factor_ref[...], preferred_element_type=jnp.float32
    )


def add_chunk(cot, gate, factor, before, weight, contract, tile):
    tokens, depth = cot.shape
    height = gate.shape[1]
    rank = factor.shape[1]
    return pl.pallas_call(
        functools.partial(chunk_kernel, contract),
        out_shape=jax.ShapeDtypeStruct((tokens, rank), jnp.float32),
        grid=(tokens // tile,),
        in_specs=[
            pl.BlockSpec((tile, depth), lambda i: (i, 0)),
            pl.BlockSpec((tile, height), lambda i: (i, 0)),
            pl.BlockSpec((height, rank), lambda i: (0, 0)),
            pl.BlockSpec((tile, rank), lambda i: (i, 0)),
            pl.BlockSpec(weight.shape, lambda i: (0, 0)),
        ],
        out_specs=pl.BlockSpec((tile, rank), lambda i: (i, 0)),
        compiler_params=pltpu.CompilerParams(vmem_limit_bytes=44 * 1024 * 1024),
        cost_estimate=pl.CostEstimate(
            flops=2 * tokens * depth * height,
            bytes_accessed=2 * (tokens * depth + height * depth + tokens * height),
            transcendentals=tokens * height,
        ),
    )(cot, gate, factor, before, weight)


def dot3(a, b, dims):
    a_high, b_high = a.astype(jnp.bfloat16), b.astype(jnp.bfloat16)
    a_low = (a - a_high.astype(jnp.float32)).astype(jnp.bfloat16)
    b_low = (b - b_high.astype(jnp.float32)).astype(jnp.bfloat16)
    dot = functools.partial(
        lax.dot_general, dimension_numbers=(dims, ((), ())), preferred_element_type=jnp.float32
    )
    return dot(a_high, b_high) + (dot(a_high, b_low) + dot(a_low, b_high))


def final_kernel(n, share, place_ref, queries_ref, *refs):
    pieces, (fisher_ref, scores_ref, every_ref) = refs[:n], refs[n:]
    docs, width = pieces[0].shape
    total = n * docs
    stage, which = place_ref[0], place_ref[1]
    for r in range(n):
        at = pl.multiple_of(lax.rem(stage + (n - r), n) * docs, docs)
        every_ref[pl.ds(at, docs), :] = pieces[r][...]
    every = every_ref[...]
    mean_diag = jnp.sum(jnp.sum(every * every, axis=1, keepdims=True), axis=0, keepdims=True) / width
    scale = 1.0 / mean_diag
    mine = every_ref[:, pl.ds(pl.multiple_of(which * share, share), share)]
    fisher_ref[...] = dot3(mine, every, ((0,), (0,))) * scale

    lanes = -(-(total + docs) // LANES) * LANES
    tall = jnp.concatenate([every, jnp.zeros((lanes - total, width), jnp.float32)], axis=0)
    row = lax.broadcasted_iota(jnp.int32, (total, lanes), 0)
    lane = lax.broadcasted_iota(jnp.int32, (total, lanes), 1)
    own = (lane >= total) & (lane - total == row - stage * docs) & (lane < total + docs)
    table = dot3(every, tall, ((1,), (1,))) * scale + jnp.where((lane == row) | own, 1.0, 0.0)
    products = dot3(every, queries_ref[...], ((1,), (1,)))

    def pick(condition, x, axis):
        return jnp.sum(jnp.where(condition, x, 0.0), axis=axis, keepdims=True)

    def step(i, table):
        k = 2 * i
        left0 = pick(lane == k, table, 1)
        left1 = pick(lane == k + 1, table, 1)
        top0 = pick(row == k, table, 0)
        top1 = pick(row == k + 1, table, 0)
        column = row[:, :1]
        a = pick(column == k, left0, 0)
        b = pick(column == k, left1, 0)
        c = pick(column == k + 1, left0, 0)
        d = pick(column == k + 1, left1, 0)
        inverse = 1.0 / (a * d - b * c)
        new0 = (d * top0 - b * top1) * inverse
        new1 = (a * top1 - c * top0) * inverse
        table = table - left0 * new0 - left1 * new1
        return jnp.where(row == k, new0, jnp.where(row == k + 1, new1, table))

    table = lax.fori_loop(0, total // 2, step, table)
    scores_ref[...] = dot3(table, products, ((0,), (0,)))[total:total + docs]


def finish(stage, which, share, queries, pieces):
    n = len(pieces)
    docs, width = pieces[0].shape
    in_vmem = pl.BlockSpec(memory_space=pltpu.VMEM)
    return pl.pallas_call(
        functools.partial(final_kernel, n, share),
        out_shape=(
            jax.ShapeDtypeStruct((share, width), jnp.float32),
            jax.ShapeDtypeStruct((docs, queries.shape[0]), jnp.float32),
        ),
        in_specs=[pl.BlockSpec(memory_space=pltpu.SMEM)] + [in_vmem] * (n + 1),
        out_specs=(in_vmem, in_vmem),
        scratch_shapes=[pltpu.VMEM((n * docs, width), jnp.float32)],
        compiler_params=pltpu.CompilerParams(vmem_limit_bytes=32 * 1024 * 1024),
    )(jnp.stack([stage, which]).astype(jnp.int32), queries, *pieces)


def on_device(inputs, cotangent, gate_pre, down_weight, proj_in, proj_out, doc_lens, queries):
    n_groups, n_seq = lax.axis_size("groups"), lax.axis_size("seq")
    n_dp, n_tensor = lax.axis_size("dp"), lax.axis_size("tensor")
    group, half = lax.axis_index("groups"), lax.axis_index("seq")
    stage, side = lax.axis_index("dp"), lax.axis_index("tensor")
    rows = inputs.shape[0]
    units = gate_pre.shape[1]
    docs = doc_lens.shape[1]
    rank = proj_in.shape[1]
    width = rank * rank
    part = units // (n_groups * n_seq)
    pair = ("groups", "seq")
    sizes = (n_groups, n_seq)
    mine = group * n_seq + half

    early = lax.all_gather(
        lax.dynamic_slice_in_dim(down_weight, mine * part + LAST, part - LAST, 0), "dp", axis=1, tiled=True
    )
    piece = lax.dynamic_slice_in_dim(down_weight, mine * part, LAST, 0).T
    piece, early = lax.optimization_barrier((piece, early))
    late = lax.all_gather(piece, "dp", axis=0, tiled=True)

    order = [(dg, ds) for dg in range(n_groups) for ds in range(n_seq)]
    right = sum_over(jnp.dot(inputs, proj_in, preferred_element_type=jnp.float32), "tensor")
    rights = [right if dg == ds == 0 else shifted(right, pair, sizes, (dg, ds)) for dg, ds in order]
    lens = [doc_lens if dg == 0 else shifted(doc_lens, "groups", (n_groups,), (dg,)) for dg in range(n_groups)]
    rights, lens, cotangent, gate_pre = lax.optimization_barrier((rights, lens, cotangent, gate_pre))

    cot = jnp.zeros((len(order) * rows, n_tensor * cotangent.shape[1]), cotangent.dtype)
    gate_late = jnp.zeros((len(order) * rows, LAST), gate_pre.dtype)
    gate_early = jnp.zeros((len(order) * rows, part - LAST), gate_pre.dtype)
    placed = []
    for dg in range(n_groups):
        own = cotangent if dg == 0 else shifted(cotangent, "groups", (n_groups,), (dg,))
        pieces = [own if r == 0 else shifted(own, "tensor", (n_tensor,), (r,)) for r in range(n_tensor)]
        for ds in range(n_seq):
            for r, piece in enumerate(pieces):
                moved = piece if ds == 0 else shifted(piece, "seq", (n_seq,), (ds,))
                placed.append((ds, dg, r, moved))
    for ds, dg, r, piece in sorted(placed, key=lambda p: p[:3]):
        at = ((side - r) % n_tensor) * piece.shape[1]
        cot = lax.dynamic_update_slice(cot, piece, ((dg * n_seq + ds) * rows, at))
    for number, (dg, ds) in enumerate(order):
        to = ((group + dg) % n_groups) * n_seq + (half + ds) % n_seq
        columns = lax.dynamic_slice_in_dim(gate_pre, to * part, part, 1)
        piece = columns if dg == ds == 0 else shifted(columns, pair, sizes, (dg, ds))
        gate_late = lax.dynamic_update_slice(gate_late, piece[:, :LAST], (number * rows, 0))
        gate_early = lax.dynamic_update_slice(gate_early, piece[:, LAST:], (number * rows, 0))

    out_factor = lax.dynamic_slice_in_dim(proj_out, mine * part, part, 0)
    left = jnp.zeros((n_groups * n_seq * rows, rank), jnp.float32)
    left = add_chunk(cot, gate_early, out_factor[LAST:], left, early, 1, rows)
    left = add_chunk(cot, gate_late, out_factor[:LAST], left, late, 0, rows)

    parts = []
    for dg in range(n_groups):
        ends = jnp.cumsum(lens[dg][0])
        position = jnp.concatenate(
            [((half - ds) % n_seq) * rows + jnp.arange(rows, dtype=jnp.int32) for ds in range(n_seq)]
        )
        document = jnp.sum((position[:, None] >= ends[None, :]).astype(jnp.int32), axis=1)
        onehot = (document[:, None] == jnp.arange(docs, dtype=jnp.int32)[None, :]).astype(jnp.float32)
        span = slice(dg * n_seq * rows, (dg + 1) * n_seq * rows)
        right_block = jnp.concatenate(rights[dg * n_seq:(dg + 1) * n_seq], axis=0)
        grads = jnp.einsum(
            "tc,ti,tj->cij", onehot, left[span], right_block, precision=HIGHEST
        ).reshape(docs, width)
        parts.append(grads)
    grads = parts[0]
    for dg in range(1, n_groups):
        grads = grads + shifted(parts[dg], "groups", (n_groups,), (-dg,))
    doc_grads = sum_over(sum_over(grads, "tensor"), "seq")

    stages = [doc_grads if r == 0 else shifted(doc_grads, "dp", (n_dp,), (r,)) for r in range(n_dp)]
    share = width // (n_tensor * n_seq)
    fisher_rows, scores = finish(stage, side * n_seq + half, share, queries, stages)
    return (doc_grads, fisher_rows, scores.T)


def solution(mesh):
    return jax.shard_map(
        on_device,
        mesh=mesh,
        in_specs=(
            P(("groups", "dp", "seq"), "tensor"),
            P(("groups", "dp", "seq"), "tensor"),
            P(("groups", "dp", "seq"), "tensor"),
            P("tensor", "dp"),
            P("tensor", None),
            P("tensor", None),
            P(("groups", "dp"), None),
            P(),
        ),
        out_specs=(
            P(("groups", "dp"), None),
            P(("groups", "tensor", "seq"), None),
            P(None, ("groups", "dp")),
        ),
        check_vma=False,
    )
```

```python
import functools

import jax
import jax.numpy as jnp
from jax import lax
from jax.experimental import pallas as pl
from jax.experimental.pallas import tpu as pltpu
from jax.sharding import PartitionSpec as P

HIGHEST = lax.Precision.HIGHEST
LATE = 256
LANES = 128


def shifted(x, axes, sizes, shift):
    if isinstance(axes, str):
        (n,) = sizes
        pairs = [(i, (i + shift[0]) % n) for i in range(n)]
    else:
        a, b = sizes
        pairs = [
            (i * b + j, ((i + shift[0]) % a) * b + (j + shift[1]) % b)
            for i in range(a) for j in range(b)
        ]
    return lax.ppermute(x, axes, pairs)


def in_order(pieces, axis, dim):
    n = len(pieces)
    me = lax.axis_index(axis)
    shape = list(pieces[0].shape)
    size = shape[dim]
    shape[dim] *= n
    out = jnp.zeros(shape, pieces[0].dtype)
    for r, piece in enumerate(pieces):
        out = lax.dynamic_update_slice_in_dim(out, piece, ((me - r) % n) * size, dim)
    return out


def gather_in_order(x, axis, dim):
    n = lax.axis_size(axis)
    return in_order([x if r == 0 else shifted(x, axis, (n,), (r,)) for r in range(n)], axis, dim)


def sum_over(x, axis):
    n = lax.axis_size(axis)
    if n == 2:
        return x + shifted(x, axis, (2,), (1,))
    return jnp.sum(gather_in_order(x[None], axis, 0), axis=0)


def chunk_kernel(n, skip, me_ref, cot_ref, gate_ref, factor_ref, before_ref, *rest):
    slots, after_ref = rest[:n], rest[n]
    height, columns = slots[0].shape
    hidden = None
    for r in range(n):
        owner = lax.rem(me_ref[0] + (n - r), n)
        block = cot_ref[:, pl.ds(pl.multiple_of(owner * columns, columns), columns)]
        term = lax.dot_general(
            block, slots[r][...], (((1,), (1,)), ((), ())), preferred_element_type=jnp.float32
        )
        hidden = term if hidden is None else hidden + term
    gate = gate_ref[:, skip:skip + height].astype(jnp.float32)
    up_grad = (hidden * (gate / (1.0 + jnp.exp(-gate)))).astype(jnp.bfloat16)
    after_ref[...] = before_ref[...] + jnp.dot(
        up_grad, factor_ref[...], preferred_element_type=jnp.float32
    )


def add_chunk(me, cot, gate, low, factor, before, slots, tile):
    tokens, depth = cot.shape
    height, rank = factor.shape
    aligned = low % height == 0 and height % LANES == 0
    width, skip = (height, 0) if aligned else (gate.shape[1], low)
    at = low // height if aligned else 0
    n = len(slots)
    return pl.pallas_call(
        functools.partial(chunk_kernel, n, skip),
        out_shape=jax.ShapeDtypeStruct((tokens, rank), jnp.float32),
        grid_spec=pltpu.PrefetchScalarGridSpec(
            num_scalar_prefetch=1,
            grid=(tokens // tile,),
            in_specs=[
                pl.BlockSpec((tile, depth), lambda i, me: (i, 0)),
                pl.BlockSpec((tile, width), lambda i, me: (i, at)),
                pl.BlockSpec((height, rank), lambda i, me: (0, 0)),
                pl.BlockSpec((tile, rank), lambda i, me: (i, 0)),
            ] + [pl.BlockSpec(slots[0].shape, lambda i, me: (0, 0))] * n,
            out_specs=pl.BlockSpec((tile, rank), lambda i, me: (i, 0)),
        ),
        compiler_params=pltpu.CompilerParams(vmem_limit_bytes=36 * 1024 * 1024),
        cost_estimate=pl.CostEstimate(
            flops=2 * tokens * depth * height,
            bytes_accessed=2 * (tokens * depth + height * depth + tokens * height),
            transcendentals=tokens * height,
        ),
    )(me, cot, gate, factor, before, *slots)


def dot3(a, b, dims):
    a_high, b_high = a.astype(jnp.bfloat16), b.astype(jnp.bfloat16)
    a_low = (a - a_high.astype(jnp.float32)).astype(jnp.bfloat16)
    b_low = (b - b_high.astype(jnp.float32)).astype(jnp.bfloat16)
    dot = functools.partial(
        lax.dot_general, dimension_numbers=(dims, ((), ())), preferred_element_type=jnp.float32
    )
    return dot(a_high, b_high) + (dot(a_high, b_low) + dot(a_low, b_high))


def final_kernel(n, share, place_ref, queries_ref, *refs):
    pieces, (fisher_ref, scores_ref, every_ref) = refs[:n], refs[n:]
    docs, width = pieces[0].shape
    total = n * docs
    stage, which = place_ref[0], place_ref[1]
    for r in range(n):
        at = pl.multiple_of(lax.rem(stage + (n - r), n) * docs, docs)
        every_ref[pl.ds(at, docs), :] = pieces[r][...]
    every = every_ref[...]
    mean_diag = jnp.sum(jnp.sum(every * every, axis=1, keepdims=True), axis=0, keepdims=True) / width
    scale = 1.0 / mean_diag
    mine = every_ref[:, pl.ds(pl.multiple_of(which * share, share), share)]
    fisher_ref[...] = dot3(mine, every, ((0,), (0,))) * scale

    lanes = -(-(total + docs) // LANES) * LANES
    tall = jnp.concatenate([every, jnp.zeros((lanes - total, width), jnp.float32)], axis=0)
    row = lax.broadcasted_iota(jnp.int32, (total, lanes), 0)
    lane = lax.broadcasted_iota(jnp.int32, (total, lanes), 1)
    own = (lane >= total) & (lane - total == row - stage * docs) & (lane < total + docs)
    table = dot3(every, tall, ((1,), (1,))) * scale + jnp.where((lane == row) | own, 1.0, 0.0)
    products = dot3(every, queries_ref[...], ((1,), (1,)))

    def pick(condition, x, axis):
        return jnp.sum(jnp.where(condition, x, 0.0), axis=axis, keepdims=True)

    def step(i, table):
        k = 2 * i
        left0 = pick(lane == k, table, 1)
        left1 = pick(lane == k + 1, table, 1)
        top0 = pick(row == k, table, 0)
        top1 = pick(row == k + 1, table, 0)
        column = row[:, :1]
        a = pick(column == k, left0, 0)
        b = pick(column == k, left1, 0)
        c = pick(column == k + 1, left0, 0)
        d = pick(column == k + 1, left1, 0)
        inverse = 1.0 / (a * d - b * c)
        new0 = (d * top0 - b * top1) * inverse
        new1 = (a * top1 - c * top0) * inverse
        table = table - left0 * new0 - left1 * new1
        return jnp.where(row == k, new0, jnp.where(row == k + 1, new1, table))

    table = lax.fori_loop(0, total // 2, step, table)
    scores_ref[...] = dot3(table, products, ((0,), (0,)))[total:total + docs]


def finish(stage, which, share, queries, pieces):
    n = len(pieces)
    docs, width = pieces[0].shape
    in_vmem = pl.BlockSpec(memory_space=pltpu.VMEM)
    return pl.pallas_call(
        functools.partial(final_kernel, n, share),
        out_shape=(
            jax.ShapeDtypeStruct((share, width), jnp.float32),
            jax.ShapeDtypeStruct((docs, queries.shape[0]), jnp.float32),
        ),
        in_specs=[pl.BlockSpec(memory_space=pltpu.SMEM)] + [in_vmem] * (n + 1),
        out_specs=(in_vmem, in_vmem),
        scratch_shapes=[pltpu.VMEM((n * docs, width), jnp.float32)],
        compiler_params=pltpu.CompilerParams(vmem_limit_bytes=32 * 1024 * 1024),
    )(jnp.stack([stage, which]).astype(jnp.int32), queries, *pieces)


def on_device(inputs, cotangent, gate_pre, down_weight, proj_in, proj_out, doc_lens, queries):
    n_groups, n_seq = lax.axis_size("groups"), lax.axis_size("seq")
    n_dp, n_tensor = lax.axis_size("dp"), lax.axis_size("tensor")
    group, half = lax.axis_index("groups"), lax.axis_index("seq")
    stage, side = lax.axis_index("dp"), lax.axis_index("tensor")
    rows = inputs.shape[0]
    units = gate_pre.shape[1]
    docs = doc_lens.shape[1]
    rank = proj_in.shape[1]
    width = rank * rank
    part = units // (n_groups * n_seq)
    pair = ("groups", "seq")
    sizes = (n_groups, n_seq)
    mine = group * n_seq + half

    passed = LATE
    spans = [(passed + LATE, part), (0, passed), (passed, passed + LATE)]
    first, ringed, last = [
        lax.dynamic_slice_in_dim(down_weight, mine * part + low, high - low, 0) for low, high in spans
    ]
    first = lax.all_gather(first, "dp", axis=1, tiled=True)
    last, first = lax.optimization_barrier((last, first))
    last = lax.all_gather(last, "dp", axis=1, tiled=True)
    ring = [ringed]
    for _ in range(n_dp - 1):
        ring.append(shifted(ring[-1], "dp", (n_dp,), (1,)))
    chunks = [[first], ring, [last]]

    order = [(dg, ds) for dg in range(n_groups) for ds in range(n_seq)]
    cot = jnp.zeros((len(order) * rows, n_tensor * cotangent.shape[1]), cotangent.dtype)
    gate = jnp.zeros((len(order) * rows, part), gate_pre.dtype)
    placed, spots = [], []
    for dg in range(n_groups):
        own = cotangent if dg == 0 else shifted(cotangent, "groups", (n_groups,), (dg,))
        pieces = [own if r == 0 else shifted(own, "tensor", (n_tensor,), (r,)) for r in range(n_tensor)]
        for ds in range(n_seq):
            for r, piece in enumerate(pieces):
                moved = piece if ds == 0 else shifted(piece, "seq", (n_seq,), (ds,))
                placed.append(moved)
                spots.append((ds, dg, r))
    moved_gates = []
    for dg, ds in order:
        to = ((group + dg) % n_groups) * n_seq + (half + ds) % n_seq
        columns = lax.dynamic_slice_in_dim(gate_pre, to * part, part, 1)
        moved_gates.append(columns if dg == ds == 0 else shifted(columns, pair, sizes, (dg, ds)))
    right_part = jnp.dot(inputs, proj_in, preferred_element_type=jnp.float32)
    right_part, doc_lens, placed, moved_gates = lax.optimization_barrier(
        (right_part, doc_lens, placed, moved_gates)
    )
    right = sum_over(right_part, "tensor")
    rights = [right if dg == ds == 0 else shifted(right, pair, sizes, (dg, ds)) for dg, ds in order]
    lens = [doc_lens if dg == 0 else shifted(doc_lens, "groups", (n_groups,), (dg,)) for dg in range(n_groups)]

    for (ds, dg, r), piece in sorted(zip(spots, placed), key=lambda p: p[0]):
        at = ((side - r) % n_tensor) * piece.shape[1]
        cot = lax.dynamic_update_slice(cot, piece, ((dg * n_seq + ds) * rows, at))
    for number, piece in enumerate(moved_gates):
        gate = lax.dynamic_update_slice(gate, piece, (number * rows, 0))

    out_factor = lax.dynamic_slice_in_dim(proj_out, mine * part, part, 0)
    left = jnp.zeros((n_groups * n_seq * rows, rank), jnp.float32)
    me = jnp.reshape(stage, (1,)).astype(jnp.int32)
    for slots, (low, high) in zip(chunks, spans):
        left = add_chunk(me, cot, gate, low, out_factor[low:high], left, slots, rows)

    parts = []
    for dg in range(n_groups):
        ends = jnp.cumsum(lens[dg][0])
        position = jnp.concatenate(
            [((half - ds) % n_seq) * rows + jnp.arange(rows, dtype=jnp.int32) for ds in range(n_seq)]
        )
        document = jnp.sum((position[:, None] >= ends[None, :]).astype(jnp.int32), axis=1)
        onehot = (document[:, None] == jnp.arange(docs, dtype=jnp.int32)[None, :]).astype(jnp.float32)
        span = slice(dg * n_seq * rows, (dg + 1) * n_seq * rows)
        right_block = jnp.concatenate(rights[dg * n_seq:(dg + 1) * n_seq], axis=0)
        grads = jnp.einsum(
            "tc,ti,tj->cij", onehot, left[span], right_block, precision=HIGHEST
        ).reshape(docs, width)
        parts.append(grads)
    grads = parts[0]
    for dg in range(1, n_groups):
        grads = grads + shifted(parts[dg], "groups", (n_groups,), (-dg,))
    doc_grads = sum_over(sum_over(grads, "tensor"), "seq")

    stages = [doc_grads if r == 0 else shifted(doc_grads, "dp", (n_dp,), (r,)) for r in range(n_dp)]
    share = width // (n_tensor * n_seq)
    fisher_rows, scores = finish(stage, side * n_seq + half, share, queries, stages)
    return (doc_grads, fisher_rows, scores.T)


def solution(mesh):
    return jax.shard_map(
        on_device,
        mesh=mesh,
        in_specs=(
            P(("groups", "dp", "seq"), "tensor"),
            P(("groups", "dp", "seq"), "tensor"),
            P(("groups", "dp", "seq"), "tensor"),
            P("tensor", "dp"),
            P("tensor", None),
            P("tensor", None),
            P(("groups", "dp"), None),
            P(),
        ),
        out_specs=(
            P(("groups", "dp"), None),
            P(("groups", "tensor", "seq"), None),
            P(None, ("groups", "dp")),
        ),
        check_vma=False,
    )
```

```python
import functools

import jax
import jax.numpy as jnp
from jax import lax
from jax.experimental import pallas as pl
from jax.experimental.pallas import tpu as pltpu
from jax.sharding import PartitionSpec as P

HIGHEST = lax.Precision.HIGHEST
CUTS = (0, 512, 768, 1024)
LANES = 128


def shifted(x, axes, sizes, shift):
    if isinstance(axes, str):
        (n,) = sizes
        pairs = [(i, (i + shift[0]) % n) for i in range(n)]
    else:
        a, b = sizes
        pairs = [
            (i * b + j, ((i + shift[0]) % a) * b + (j + shift[1]) % b)
            for i in range(a) for j in range(b)
        ]
    return lax.ppermute(x, axes, pairs)


def in_order(pieces, axis, dim):
    n = len(pieces)
    me = lax.axis_index(axis)
    shape = list(pieces[0].shape)
    size = shape[dim]
    shape[dim] *= n
    out = jnp.zeros(shape, pieces[0].dtype)
    for r, piece in enumerate(pieces):
        out = lax.dynamic_update_slice_in_dim(out, piece, ((me - r) % n) * size, dim)
    return out


def gather_in_order(x, axis, dim):
    n = lax.axis_size(axis)
    return in_order([x if r == 0 else shifted(x, axis, (n,), (r,)) for r in range(n)], axis, dim)


def sum_over(x, axis):
    n = lax.axis_size(axis)
    if n == 2:
        return x + shifted(x, axis, (2,), (1,))
    return jnp.sum(gather_in_order(x[None], axis, 0), axis=0)


def chunk_kernel(n, skip, me_ref, cot_ref, gate_ref, factor_ref, before_ref, *rest):
    slots, after_ref = rest[:n], rest[n]
    height, columns = slots[0].shape
    hidden = None
    for r in range(n):
        owner = lax.rem(me_ref[0] + (n - r), n)
        block = cot_ref[:, pl.ds(pl.multiple_of(owner * columns, columns), columns)]
        term = lax.dot_general(
            block, slots[r][...], (((1,), (1,)), ((), ())), preferred_element_type=jnp.float32
        )
        hidden = term if hidden is None else hidden + term
    gate = gate_ref[:, skip:skip + height].astype(jnp.float32)
    up_grad = (hidden * (gate / (1.0 + jnp.exp(-gate)))).astype(jnp.bfloat16)
    after_ref[...] = before_ref[...] + jnp.dot(
        up_grad, factor_ref[...], preferred_element_type=jnp.float32
    )


def add_chunk(me, cot, gate, low, factor, before, slots, tile):
    tokens, depth = cot.shape
    height, rank = factor.shape
    aligned = low % height == 0 and height % LANES == 0
    width, skip = (height, 0) if aligned else (gate.shape[1], low)
    at = low // height if aligned else 0
    n = len(slots)
    columns = slots[0].shape[1]
    if low % height:
        slots = [slot if slot.shape[0] == height else slot[low:low + height] for slot in slots]

    def weight_spec(slot):
        block = 0 if slot.shape[0] == height else low // height
        return pl.BlockSpec((height, columns), lambda i, me: (block, 0))

    return pl.pallas_call(
        functools.partial(chunk_kernel, n, skip),
        out_shape=jax.ShapeDtypeStruct((tokens, rank), jnp.float32),
        grid_spec=pltpu.PrefetchScalarGridSpec(
            num_scalar_prefetch=1,
            grid=(tokens // tile,),
            in_specs=[
                pl.BlockSpec((tile, depth), lambda i, me: (i, 0)),
                pl.BlockSpec((tile, width), lambda i, me: (i, at)),
                pl.BlockSpec((height, rank), lambda i, me: (0, 0)),
                pl.BlockSpec((tile, rank), lambda i, me: (i, 0)),
            ] + [weight_spec(slot) for slot in slots],
            out_specs=pl.BlockSpec((tile, rank), lambda i, me: (i, 0)),
        ),
        compiler_params=pltpu.CompilerParams(vmem_limit_bytes=36 * 1024 * 1024),
        cost_estimate=pl.CostEstimate(
            flops=2 * tokens * depth * height,
            bytes_accessed=2 * (tokens * depth + height * depth + tokens * height),
            transcendentals=tokens * height,
        ),
    )(me, cot, gate, factor, before, *slots)


def dot3(a, b, dims):
    a_high, b_high = a.astype(jnp.bfloat16), b.astype(jnp.bfloat16)
    a_low = (a - a_high.astype(jnp.float32)).astype(jnp.bfloat16)
    b_low = (b - b_high.astype(jnp.float32)).astype(jnp.bfloat16)
    dot = functools.partial(
        lax.dot_general, dimension_numbers=(dims, ((), ())), preferred_element_type=jnp.float32
    )
    return dot(a_high, b_high) + (dot(a_high, b_low) + dot(a_low, b_high))


def final_kernel(n, share, place_ref, queries_ref, *refs):
    pieces, (fisher_ref, scores_ref, every_ref) = refs[:n], refs[n:]
    docs, width = pieces[0].shape
    total = n * docs
    stage, which = place_ref[0], place_ref[1]
    for r in range(n):
        at = pl.multiple_of(lax.rem(stage + (n - r), n) * docs, docs)
        every_ref[pl.ds(at, docs), :] = pieces[r][...]
    every = every_ref[...]
    mean_diag = jnp.sum(jnp.sum(every * every, axis=1, keepdims=True), axis=0, keepdims=True) / width
    scale = 1.0 / mean_diag
    mine = every_ref[:, pl.ds(pl.multiple_of(which * share, share), share)]
    fisher_ref[...] = dot3(mine, every, ((0,), (0,))) * scale

    lanes = -(-(total + docs) // LANES) * LANES
    tall = jnp.concatenate([every, jnp.zeros((lanes - total, width), jnp.float32)], axis=0)
    row = lax.broadcasted_iota(jnp.int32, (total, lanes), 0)
    lane = lax.broadcasted_iota(jnp.int32, (total, lanes), 1)
    own = (lane >= total) & (lane - total == row - stage * docs) & (lane < total + docs)
    table = dot3(every, tall, ((1,), (1,))) * scale + jnp.where((lane == row) | own, 1.0, 0.0)
    products = dot3(every, queries_ref[...], ((1,), (1,)))

    def pick(condition, x, axis):
        return jnp.sum(jnp.where(condition, x, 0.0), axis=axis, keepdims=True)

    def step(i, table):
        k = 2 * i
        left0 = pick(lane == k, table, 1)
        left1 = pick(lane == k + 1, table, 1)
        top0 = pick(row == k, table, 0)
        top1 = pick(row == k + 1, table, 0)
        column = row[:, :1]
        a = pick(column == k, left0, 0)
        b = pick(column == k, left1, 0)
        c = pick(column == k + 1, left0, 0)
        d = pick(column == k + 1, left1, 0)
        inverse = 1.0 / (a * d - b * c)
        new0 = (d * top0 - b * top1) * inverse
        new1 = (a * top1 - c * top0) * inverse
        table = table - left0 * new0 - left1 * new1
        return jnp.where(row == k, new0, jnp.where(row == k + 1, new1, table))

    table = lax.fori_loop(0, total // 2, step, table)
    scores_ref[...] = dot3(table, products, ((0,), (0,)))[total:total + docs]


def finish(stage, which, share, queries, pieces):
    n = len(pieces)
    docs, width = pieces[0].shape
    in_vmem = pl.BlockSpec(memory_space=pltpu.VMEM)
    return pl.pallas_call(
        functools.partial(final_kernel, n, share),
        out_shape=(
            jax.ShapeDtypeStruct((share, width), jnp.float32),
            jax.ShapeDtypeStruct((docs, queries.shape[0]), jnp.float32),
        ),
        in_specs=[pl.BlockSpec(memory_space=pltpu.SMEM)] + [in_vmem] * (n + 1),
        out_specs=(in_vmem, in_vmem),
        scratch_shapes=[pltpu.VMEM((n * docs, width), jnp.float32)],
        compiler_params=pltpu.CompilerParams(vmem_limit_bytes=32 * 1024 * 1024),
    )(jnp.stack([stage, which]).astype(jnp.int32), queries, *pieces)


def on_device(inputs, cotangent, gate_pre, down_weight, proj_in, proj_out, doc_lens, queries):
    n_groups, n_seq = lax.axis_size("groups"), lax.axis_size("seq")
    n_dp, n_tensor = lax.axis_size("dp"), lax.axis_size("tensor")
    group, half = lax.axis_index("groups"), lax.axis_index("seq")
    stage, side = lax.axis_index("dp"), lax.axis_index("tensor")
    rows = inputs.shape[0]
    units = gate_pre.shape[1]
    docs = doc_lens.shape[1]
    rank = proj_in.shape[1]
    width = rank * rank
    part = units // (n_groups * n_seq)
    pair = ("groups", "seq")
    sizes = (n_groups, n_seq)
    mine = group * n_seq + half

    lows = [low for low in CUTS if low < part]
    spans = list(zip(lows, lows[1:] + [part]))
    spans = spans[:1] + spans[3:] + spans[1:3]
    ring = [lax.dynamic_slice_in_dim(down_weight, mine * part, part, 0)]

    def across(x, ds):
        return shifted(x, "seq", (n_seq,), (ds,))

    order = [(dg, ds) for dg in range(n_groups) for ds in range(n_seq)]

    def unit_columns(dg, ds):
        to = ((group + dg) % n_groups) * n_seq + (half + ds) % n_seq
        return lax.dynamic_slice_in_dim(gate_pre, to * part, part, 1)

    cots = {(0, 0, 0): cotangent}
    for dg in range(1, n_groups):
        cots[dg, 0, 0] = shifted(cotangent, "groups", (n_groups,), (dg,))
    for r in range(1, n_tensor):
        cots[0, 0, r] = shifted(cotangent, "tensor", (n_tensor,), (r,))
    sheets = {
        dg: jnp.concatenate([unit_columns(dg, ds) for ds in range(n_seq)], axis=0)
        for dg in range(n_groups)
    }
    for dg in range(1, n_groups):
        sheets[dg] = shifted(sheets[dg], "groups", (n_groups,), (dg,))
    turned = shifted(ring[-1], "dp", (n_dp,), (1,))
    turned, cots = lax.optimization_barrier((turned, cots))
    ring.append(turned)

    gates, more = {}, {}

    def spread(dg, sheet):
        for ds in range(n_seq):
            x = sheet[ds * rows:(ds + 1) * rows]
            gates[dg, ds] = x if ds == 0 else across(x, ds)

    spread(0, sheets[0])
    for (dg, _, r), x in cots.items():
        for ds in range(1, n_seq):
            more[dg, ds, r] = across(x, ds)
    for dg in range(1, n_groups):
        for r in range(1, n_tensor):
            more[dg, 0, r] = shifted(cots[dg, 0, 0], "tensor", (n_tensor,), (r,))
    right_part = jnp.dot(inputs, proj_in, preferred_element_type=jnp.float32)
    turned = shifted(ring[-1], "dp", (n_dp,), (1,)) if n_dp > 3 else ring.pop()
    turned, cots, more, sheets, right_part, doc_lens = lax.optimization_barrier(
        (turned, cots, more, sheets, right_part, doc_lens)
    )
    ring.append(turned)
    cots.update(more)

    for dg in range(1, n_groups):
        for r in range(1, n_tensor):
            for ds in range(1, n_seq):
                cots[dg, ds, r] = across(cots[dg, 0, r], ds)
        spread(dg, sheets[dg])
    while len(ring) < n_dp - 1:
        ring.append(shifted(ring[-1], "dp", (n_dp,), (1,)))
    chunks = [
        ring + ([shifted(ring[-1][low:high], "dp", (n_dp,), (1,))] if n_dp > 1 else [])
        for low, high in spans
    ]
    right = sum_over(right_part, "tensor")
    rights = [right if dg == ds == 0 else shifted(right, pair, sizes, (dg, ds)) for dg, ds in order]
    lens = [doc_lens if dg == 0 else shifted(doc_lens, "groups", (n_groups,), (dg,)) for dg in range(n_groups)]

    cot = jnp.zeros((len(order) * rows, n_tensor * cotangent.shape[1]), cotangent.dtype)
    gate = jnp.zeros((len(order) * rows, part), gate_pre.dtype)
    for (dg, ds, r), block in sorted(cots.items(), key=lambda item: (item[0][1] * item[0][0] * item[0][2], item[0])):
        at = ((side - r) % n_tensor) * cotangent.shape[1]
        cot = lax.dynamic_update_slice(cot, block, ((dg * n_seq + ds) * rows, at))
    for number, place in enumerate(order):
        gate = lax.dynamic_update_slice(gate, gates[place], (number * rows, 0))

    out_factor = lax.dynamic_slice_in_dim(proj_out, mine * part, part, 0)
    left = jnp.zeros((n_groups * n_seq * rows, rank), jnp.float32)
    me = jnp.reshape(stage, (1,)).astype(jnp.int32)
    for slots, (low, high) in zip(chunks, spans):
        left = add_chunk(me, cot, gate, low, out_factor[low:high], left, slots, rows)

    parts = []
    for dg in range(n_groups):
        ends = jnp.cumsum(lens[dg][0])
        position = jnp.concatenate(
            [((half - ds) % n_seq) * rows + jnp.arange(rows, dtype=jnp.int32) for ds in range(n_seq)]
        )
        document = jnp.sum((position[:, None] >= ends[None, :]).astype(jnp.int32), axis=1)
        onehot = (document[:, None] == jnp.arange(docs, dtype=jnp.int32)[None, :]).astype(jnp.float32)
        span = slice(dg * n_seq * rows, (dg + 1) * n_seq * rows)
        right_block = jnp.concatenate(rights[dg * n_seq:(dg + 1) * n_seq], axis=0)
        grads = jnp.einsum(
            "tc,ti,tj->cij", onehot, left[span], right_block, precision=HIGHEST
        ).reshape(docs, width)
        parts.append(grads)
    grads = parts[0]
    for dg in range(1, n_groups):
        grads = grads + shifted(parts[dg], "groups", (n_groups,), (-dg,))
    doc_grads = sum_over(sum_over(grads, "tensor"), "seq")

    stages = [doc_grads if r == 0 else shifted(doc_grads, "dp", (n_dp,), (r,)) for r in range(n_dp)]
    share = width // (n_tensor * n_seq)
    fisher_rows, scores = finish(stage, side * n_seq + half, share, queries, stages)
    return (doc_grads, fisher_rows, scores.T)


def solution(mesh):
    return jax.shard_map(
        on_device,
        mesh=mesh,
        in_specs=(
            P(("groups", "dp", "seq"), "tensor"),
            P(("groups", "dp", "seq"), "tensor"),
            P(("groups", "dp", "seq"), "tensor"),
            P("tensor", "dp"),
            P("tensor", None),
            P("tensor", None),
            P(("groups", "dp"), None),
            P(),
        ),
        out_specs=(
            P(("groups", "dp"), None),
            P(("groups", "tensor", "seq"), None),
            P(None, ("groups", "dp")),
        ),
        check_vma=False,
    )
```

```python
import functools

import jax
import jax.numpy as jnp
from jax import lax
from jax.experimental import pallas as pl
from jax.experimental.pallas import tpu as pltpu
from jax.sharding import PartitionSpec as P

HIGHEST = lax.Precision.HIGHEST
CUTS = (0, 512, 768, 1024)
LANES = 128


def shifted(x, axes, sizes, shift):
    if isinstance(axes, str):
        (n,) = sizes
        pairs = [(i, (i + shift[0]) % n) for i in range(n)]
    else:
        a, b = sizes
        pairs = [
            (i * b + j, ((i + shift[0]) % a) * b + (j + shift[1]) % b)
            for i in range(a) for j in range(b)
        ]
    return lax.ppermute(x, axes, pairs)


def in_order(pieces, axis, dim):
    n = len(pieces)
    me = lax.axis_index(axis)
    shape = list(pieces[0].shape)
    size = shape[dim]
    shape[dim] *= n
    out = jnp.zeros(shape, pieces[0].dtype)
    for r, piece in enumerate(pieces):
        out = lax.dynamic_update_slice_in_dim(out, piece, ((me - r) % n) * size, dim)
    return out


def gather_in_order(x, axis, dim):
    n = lax.axis_size(axis)
    return in_order([x if r == 0 else shifted(x, axis, (n,), (r,)) for r in range(n)], axis, dim)


def sum_over(x, axis):
    n = lax.axis_size(axis)
    if n == 2:
        return x + shifted(x, axis, (2,), (1,))
    return jnp.sum(gather_in_order(x[None], axis, 0), axis=0)


def chunk_kernel(n, skip, me_ref, cot_ref, gate_ref, factor_ref, before_ref, *rest):
    slots, after_ref = rest[:n], rest[n]
    height, columns = slots[0].shape
    hidden = None
    for r in range(n):
        owner = lax.rem(me_ref[0] + (n - r), n)
        block = cot_ref[:, pl.ds(pl.multiple_of(owner * columns, columns), columns)]
        term = lax.dot_general(
            block, slots[r][...], (((1,), (1,)), ((), ())), preferred_element_type=jnp.float32
        )
        hidden = term if hidden is None else hidden + term
    gate = gate_ref[:, skip:skip + height].astype(jnp.float32)
    up_grad = (hidden * (gate / (1.0 + jnp.exp(-gate)))).astype(jnp.bfloat16)
    after_ref[...] = before_ref[...] + jnp.dot(
        up_grad, factor_ref[...], preferred_element_type=jnp.float32
    )


def add_chunk(me, cot, gate, low, factor, before, slots, tile):
    tokens, depth = cot.shape
    height, rank = factor.shape
    aligned = low % height == 0 and height % LANES == 0
    width, skip = (height, 0) if aligned else (gate.shape[1], low)
    at = low // height if aligned else 0
    n = len(slots)
    columns = slots[0].shape[1]
    if low % height:
        slots = [slot if slot.shape[0] == height else slot[low:low + height] for slot in slots]

    def weight_spec(slot):
        block = 0 if slot.shape[0] == height else low // height
        return pl.BlockSpec((height, columns), lambda i, me: (block, 0))

    return pl.pallas_call(
        functools.partial(chunk_kernel, n, skip),
        out_shape=jax.ShapeDtypeStruct((tokens, rank), jnp.float32),
        grid_spec=pltpu.PrefetchScalarGridSpec(
            num_scalar_prefetch=1,
            grid=(tokens // tile,),
            in_specs=[
                pl.BlockSpec((tile, depth), lambda i, me: (i, 0)),
                pl.BlockSpec((tile, width), lambda i, me: (i, at)),
                pl.BlockSpec((height, rank), lambda i, me: (0, 0)),
                pl.BlockSpec((tile, rank), lambda i, me: (i, 0)),
            ] + [weight_spec(slot) for slot in slots],
            out_specs=pl.BlockSpec((tile, rank), lambda i, me: (i, 0)),
        ),
        compiler_params=pltpu.CompilerParams(vmem_limit_bytes=36 * 1024 * 1024),
        cost_estimate=pl.CostEstimate(
            flops=2 * tokens * depth * height,
            bytes_accessed=2 * (tokens * depth + height * depth + tokens * height),
            transcendentals=tokens * height,
        ),
    )(me, cot, gate, factor, before, *slots)


def dot3(a, b, dims):
    a_high, b_high = a.astype(jnp.bfloat16), b.astype(jnp.bfloat16)
    a_low = (a - a_high.astype(jnp.float32)).astype(jnp.bfloat16)
    b_low = (b - b_high.astype(jnp.float32)).astype(jnp.bfloat16)
    dot = functools.partial(
        lax.dot_general, dimension_numbers=(dims, ((), ())), preferred_element_type=jnp.float32
    )
    return dot(a_high, b_high) + (dot(a_high, b_low) + dot(a_low, b_high))


def final_kernel(n, share, place_ref, queries_ref, *refs):
    pieces, (fisher_ref, scores_ref, every_ref) = refs[:n], refs[n:]
    docs, width = pieces[0].shape
    total = n * docs
    stage, which = place_ref[0], place_ref[1]
    for r in range(n):
        at = pl.multiple_of(lax.rem(stage + (n - r), n) * docs, docs)
        every_ref[pl.ds(at, docs), :] = pieces[r][...]
    every = every_ref[...]
    mean_diag = jnp.sum(jnp.sum(every * every, axis=1, keepdims=True), axis=0, keepdims=True) / width
    scale = 1.0 / mean_diag
    mine = every_ref[:, pl.ds(pl.multiple_of(which * share, share), share)]
    fisher_ref[...] = dot3(mine, every, ((0,), (0,))) * scale

    lanes = -(-(total + docs) // LANES) * LANES
    tall = jnp.concatenate([every, jnp.zeros((lanes - total, width), jnp.float32)], axis=0)
    row = lax.broadcasted_iota(jnp.int32, (total, lanes), 0)
    lane = lax.broadcasted_iota(jnp.int32, (total, lanes), 1)
    own = (lane >= total) & (lane - total == row - stage * docs) & (lane < total + docs)
    table = dot3(every, tall, ((1,), (1,))) * scale + jnp.where((lane == row) | own, 1.0, 0.0)
    products = dot3(every, queries_ref[...], ((1,), (1,)))

    def pick(condition, x, axis):
        return jnp.sum(jnp.where(condition, x, 0.0), axis=axis, keepdims=True)

    def step(i, table):
        k = 2 * i
        left0 = pick(lane == k, table, 1)
        left1 = pick(lane == k + 1, table, 1)
        top0 = pick(row == k, table, 0)
        top1 = pick(row == k + 1, table, 0)
        column = row[:, :1]
        a = pick(column == k, left0, 0)
        b = pick(column == k, left1, 0)
        c = pick(column == k + 1, left0, 0)
        d = pick(column == k + 1, left1, 0)
        inverse = 1.0 / (a * d - b * c)
        new0 = (d * top0 - b * top1) * inverse
        new1 = (a * top1 - c * top0) * inverse
        table = table - left0 * new0 - left1 * new1
        return jnp.where(row == k, new0, jnp.where(row == k + 1, new1, table))

    table = lax.fori_loop(0, total // 2, step, table)
    scores_ref[...] = dot3(table, products, ((0,), (0,)))[total:total + docs]


def finish(stage, which, share, queries, pieces):
    n = len(pieces)
    docs, width = pieces[0].shape
    in_vmem = pl.BlockSpec(memory_space=pltpu.VMEM)
    return pl.pallas_call(
        functools.partial(final_kernel, n, share),
        out_shape=(
            jax.ShapeDtypeStruct((share, width), jnp.float32),
            jax.ShapeDtypeStruct((docs, queries.shape[0]), jnp.float32),
        ),
        in_specs=[pl.BlockSpec(memory_space=pltpu.SMEM)] + [in_vmem] * (n + 1),
        out_specs=(in_vmem, in_vmem),
        scratch_shapes=[pltpu.VMEM((n * docs, width), jnp.float32)],
        compiler_params=pltpu.CompilerParams(vmem_limit_bytes=32 * 1024 * 1024),
    )(jnp.stack([stage, which]).astype(jnp.int32), queries, *pieces)


def on_device(inputs, cotangent, gate_pre, down_weight, proj_in, proj_out, doc_lens, queries):
    n_groups, n_seq = lax.axis_size("groups"), lax.axis_size("seq")
    n_dp, n_tensor = lax.axis_size("dp"), lax.axis_size("tensor")
    group, half = lax.axis_index("groups"), lax.axis_index("seq")
    stage, side = lax.axis_index("dp"), lax.axis_index("tensor")
    rows = inputs.shape[0]
    units = gate_pre.shape[1]
    docs = doc_lens.shape[1]
    rank = proj_in.shape[1]
    width = rank * rank
    part = units // (n_groups * n_seq)
    pair = ("groups", "seq")
    sizes = (n_groups, n_seq)
    mine = group * n_seq + half

    lows = [low for low in CUTS if low < part]
    spans = list(zip(lows, lows[1:] + [part]))
    spans = spans[:1] + spans[3:] + spans[1:3]
    ring = [lax.dynamic_slice_in_dim(down_weight, mine * part, part, 0)]

    def across(x, ds):
        return shifted(x, "seq", (n_seq,), (ds,))

    order = [(dg, ds) for dg in range(n_groups) for ds in range(n_seq)]

    def place(cot, dg, ds, r, block):
        at = ((side - r) % n_tensor) * block.shape[1]
        return lax.dynamic_update_slice(cot, block, ((dg * n_seq + ds) * rows, at))

    def unit_columns(dg, ds):
        to = ((group + dg) % n_groups) * n_seq + (half + ds) % n_seq
        return lax.dynamic_slice_in_dim(gate_pre, to * part, part, 1)

    cots = {(0, 0, 0): cotangent}
    for dg in range(1, n_groups):
        cots[dg, 0, 0] = shifted(cotangent, "groups", (n_groups,), (dg,))
    for r in range(1, n_tensor):
        cots[0, 0, r] = shifted(cotangent, "tensor", (n_tensor,), (r,))
    sheets = {
        dg: jnp.concatenate([unit_columns(dg, ds) for ds in range(n_seq)], axis=0)
        for dg in range(n_groups)
    }
    for dg in range(1, n_groups):
        sheets[dg] = shifted(sheets[dg], "groups", (n_groups,), (dg,))
    turned = shifted(ring[-1], "dp", (n_dp,), (1,))
    turned, cots = lax.optimization_barrier((turned, cots))
    ring.append(turned)

    gates, more = {}, {}

    def spread(dg, sheet):
        for ds in range(n_seq):
            x = sheet[ds * rows:(ds + 1) * rows]
            gates[dg, ds] = x if ds == 0 else across(x, ds)

    spread(0, sheets[0])
    for (dg, _, r), x in cots.items():
        for ds in range(1, n_seq):
            more[dg, ds, r] = across(x, ds)
    for dg in range(1, n_groups):
        for r in range(1, n_tensor):
            more[dg, 0, r] = shifted(cots[dg, 0, 0], "tensor", (n_tensor,), (r,))
    right_part = jnp.dot(inputs, proj_in, preferred_element_type=jnp.float32)
    out_factor = lax.dynamic_slice_in_dim(proj_out, mine * part, part, 0)
    factors = [out_factor[low:high] for low, high in spans]
    cot = jnp.zeros((len(order) * rows, n_tensor * cotangent.shape[1]), cotangent.dtype)
    for r in range(n_tensor):
        cot = place(cot, 0, 0, r, cots[0, 0, r])
    turned = shifted(ring[-1], "dp", (n_dp,), (1,)) if n_dp > 3 else ring.pop()
    turned, cot, cots, more, sheets, right_part, doc_lens, factors = lax.optimization_barrier(
        (turned, cot, cots, more, sheets, right_part, doc_lens, factors)
    )
    ring.append(turned)
    cots.update(more)

    while len(ring) < n_dp - 1:
        ring.append(shifted(ring[-1], "dp", (n_dp,), (1,)))
    cuts = [ring[-1][low:high] for low, high in spans]
    cuts, cot, cots, sheets, right_part, doc_lens = lax.optimization_barrier(
        (cuts, cot, cots, sheets, right_part, doc_lens)
    )
    turned = [shifted(cut, "dp", (n_dp,), (1,)) for cut in cuts]
    for dg in range(1, n_groups):
        for r in range(1, n_tensor):
            for ds in range(1, n_seq):
                cots[dg, ds, r] = across(cots[dg, 0, r], ds)
        spread(dg, sheets[dg])
    chunks = [ring + [block] for block in turned]
    right = sum_over(right_part, "tensor")
    rights = [right if dg == ds == 0 else shifted(right, pair, sizes, (dg, ds)) for dg, ds in order]
    lens = [doc_lens if dg == 0 else shifted(doc_lens, "groups", (n_groups,), (dg,)) for dg in range(n_groups)]

    gate = jnp.zeros((len(order) * rows, part), gate_pre.dtype)
    for (dg, ds, r), block in sorted(cots.items(), key=lambda item: (item[0][0] * item[0][2], item[0])):
        if (dg, ds) != (0, 0):
            cot = place(cot, dg, ds, r, block)
    for number, block in enumerate(order):
        gate = lax.dynamic_update_slice(gate, gates[block], (number * rows, 0))

    left = jnp.zeros((n_groups * n_seq * rows, rank), jnp.float32)
    me = jnp.reshape(stage, (1,)).astype(jnp.int32)
    for slots, (low, high), factor in zip(chunks, spans, factors):
        left = add_chunk(me, cot, gate, low, factor, left, slots, rows)

    parts = []
    for dg in range(n_groups):
        ends = jnp.cumsum(lens[dg][0])
        position = jnp.concatenate(
            [((half - ds) % n_seq) * rows + jnp.arange(rows, dtype=jnp.int32) for ds in range(n_seq)]
        )
        document = jnp.sum((position[:, None] >= ends[None, :]).astype(jnp.int32), axis=1)
        onehot = (document[:, None] == jnp.arange(docs, dtype=jnp.int32)[None, :]).astype(jnp.float32)
        span = slice(dg * n_seq * rows, (dg + 1) * n_seq * rows)
        right_block = jnp.concatenate(rights[dg * n_seq:(dg + 1) * n_seq], axis=0)
        grads = jnp.einsum(
            "tc,ti,tj->cij", onehot, left[span], right_block, precision=HIGHEST
        ).reshape(docs, width)
        parts.append(grads)
    grads = parts[0]
    for dg in range(1, n_groups):
        grads = grads + shifted(parts[dg], "groups", (n_groups,), (-dg,))
    doc_grads = sum_over(sum_over(grads, "tensor"), "seq")

    stages = [doc_grads if r == 0 else shifted(doc_grads, "dp", (n_dp,), (r,)) for r in range(n_dp)]
    share = width // (n_tensor * n_seq)
    fisher_rows, scores = finish(stage, side * n_seq + half, share, queries, stages)
    return (doc_grads, fisher_rows, scores.T)


def solution(mesh):
    return jax.shard_map(
        on_device,
        mesh=mesh,
        in_specs=(
            P(("groups", "dp", "seq"), "tensor"),
            P(("groups", "dp", "seq"), "tensor"),
            P(("groups", "dp", "seq"), "tensor"),
            P("tensor", "dp"),
            P("tensor", None),
            P("tensor", None),
            P(("groups", "dp"), None),
            P(),
        ),
        out_specs=(
            P(("groups", "dp"), None),
            P(("groups", "tensor", "seq"), None),
            P(None, ("groups", "dp")),
        ),
        check_vma=False,
    )
```

```python
import functools

import jax
import jax.numpy as jnp
from jax import lax
from jax.experimental import pallas as pl
from jax.experimental.pallas import tpu as pltpu
from jax.sharding import PartitionSpec as P

HIGHEST = lax.Precision.HIGHEST
CUTS = (0, 512, 768, 1024)
LANES = 128


def shifted(x, axes, sizes, shift):
    if isinstance(axes, str):
        (n,) = sizes
        pairs = [(i, (i + shift[0]) % n) for i in range(n)]
    else:
        a, b = sizes
        pairs = [
            (i * b + j, ((i + shift[0]) % a) * b + (j + shift[1]) % b)
            for i in range(a) for j in range(b)
        ]
    return lax.ppermute(x, axes, pairs)


def in_order(pieces, axis, dim):
    n = len(pieces)
    me = lax.axis_index(axis)
    shape = list(pieces[0].shape)
    size = shape[dim]
    shape[dim] *= n
    out = jnp.zeros(shape, pieces[0].dtype)
    for r, piece in enumerate(pieces):
        out = lax.dynamic_update_slice_in_dim(out, piece, ((me - r) % n) * size, dim)
    return out


def gather_in_order(x, axis, dim):
    n = lax.axis_size(axis)
    return in_order([x if r == 0 else shifted(x, axis, (n,), (r,)) for r in range(n)], axis, dim)


def sum_over(x, axis):
    n = lax.axis_size(axis)
    if n == 2:
        return x + shifted(x, axis, (2,), (1,))
    return jnp.sum(gather_in_order(x[None], axis, 0), axis=0)


def chunk_kernel(n, skip, me_ref, cot_ref, gate_ref, factor_ref, before_ref, *rest):
    slots, after_ref = rest[:n], rest[n]
    height, columns = slots[0].shape
    hidden = None
    for r in range(n):
        owner = lax.rem(me_ref[0] + (n - r), n)
        block = cot_ref[:, pl.ds(pl.multiple_of(owner * columns, columns), columns)]
        term = lax.dot_general(
            block, slots[r][...], (((1,), (1,)), ((), ())), preferred_element_type=jnp.float32
        )
        hidden = term if hidden is None else hidden + term
    gate = gate_ref[:, skip:skip + height].astype(jnp.float32)
    up_grad = (hidden * (gate / (1.0 + jnp.exp(-gate)))).astype(jnp.bfloat16)
    after_ref[...] = before_ref[...] + jnp.dot(
        up_grad, factor_ref[...], preferred_element_type=jnp.float32
    )


def add_chunk(me, cot, gate, low, factor, before, slots, tile):
    tokens, depth = cot.shape
    height, rank = factor.shape
    aligned = low % height == 0 and height % LANES == 0
    width, skip = (height, 0) if aligned else (gate.shape[1], low)
    at = low // height if aligned else 0
    n = len(slots)
    columns = slots[0].shape[1]
    if low % height:
        slots = [slot if slot.shape[0] == height else slot[low:low + height] for slot in slots]

    def weight_spec(slot):
        block = 0 if slot.shape[0] == height else low // height
        return pl.BlockSpec((height, columns), lambda i, me: (block, 0))

    return pl.pallas_call(
        functools.partial(chunk_kernel, n, skip),
        out_shape=jax.ShapeDtypeStruct((tokens, rank), jnp.float32),
        grid_spec=pltpu.PrefetchScalarGridSpec(
            num_scalar_prefetch=1,
            grid=(tokens // tile,),
            in_specs=[
                pl.BlockSpec((tile, depth), lambda i, me: (i, 0)),
                pl.BlockSpec((tile, width), lambda i, me: (i, at)),
                pl.BlockSpec((height, rank), lambda i, me: (0, 0)),
                pl.BlockSpec((tile, rank), lambda i, me: (i, 0)),
            ] + [weight_spec(slot) for slot in slots],
            out_specs=pl.BlockSpec((tile, rank), lambda i, me: (i, 0)),
        ),
        compiler_params=pltpu.CompilerParams(vmem_limit_bytes=36 * 1024 * 1024),
        cost_estimate=pl.CostEstimate(
            flops=2 * tokens * depth * height,
            bytes_accessed=2 * (tokens * depth + height * depth + tokens * height),
            transcendentals=tokens * height,
        ),
    )(me, cot, gate, factor, before, *slots)


def dot3(a, b, dims):
    a_high, b_high = a.astype(jnp.bfloat16), b.astype(jnp.bfloat16)
    a_low = (a - a_high.astype(jnp.float32)).astype(jnp.bfloat16)
    b_low = (b - b_high.astype(jnp.float32)).astype(jnp.bfloat16)
    dot = functools.partial(
        lax.dot_general, dimension_numbers=(dims, ((), ())), preferred_element_type=jnp.float32
    )
    return dot(a_high, b_high) + (dot(a_high, b_low) + dot(a_low, b_high))


def final_kernel(n, share, place_ref, queries_ref, *refs):
    pieces, (fisher_ref, scores_ref, every_ref) = refs[:n], refs[n:]
    docs, width = pieces[0].shape
    total = n * docs
    stage, which = place_ref[0], place_ref[1]
    for r in range(n):
        at = pl.multiple_of(lax.rem(stage + (n - r), n) * docs, docs)
        every_ref[pl.ds(at, docs), :] = pieces[r][...]
    every = every_ref[...]
    mean_diag = jnp.sum(jnp.sum(every * every, axis=1, keepdims=True), axis=0, keepdims=True) / width
    scale = 1.0 / mean_diag
    mine = every_ref[:, pl.ds(pl.multiple_of(which * share, share), share)]
    fisher_ref[...] = dot3(mine, every, ((0,), (0,))) * scale

    lanes = -(-(total + docs) // LANES) * LANES
    tall = jnp.concatenate([every, jnp.zeros((lanes - total, width), jnp.float32)], axis=0)
    row = lax.broadcasted_iota(jnp.int32, (total, lanes), 0)
    lane = lax.broadcasted_iota(jnp.int32, (total, lanes), 1)
    own = (lane >= total) & (lane - total == row - stage * docs) & (lane < total + docs)
    table = dot3(every, tall, ((1,), (1,))) * scale + jnp.where((lane == row) | own, 1.0, 0.0)
    products = dot3(every, queries_ref[...], ((1,), (1,)))

    def pick(condition, x, axis):
        return jnp.sum(jnp.where(condition, x, 0.0), axis=axis, keepdims=True)

    def step(i, table):
        k = 2 * i
        left0 = pick(lane == k, table, 1)
        left1 = pick(lane == k + 1, table, 1)
        top0 = pick(row == k, table, 0)
        top1 = pick(row == k + 1, table, 0)
        column = row[:, :1]
        a = pick(column == k, left0, 0)
        b = pick(column == k, left1, 0)
        c = pick(column == k + 1, left0, 0)
        d = pick(column == k + 1, left1, 0)
        inverse = 1.0 / (a * d - b * c)
        new0 = (d * top0 - b * top1) * inverse
        new1 = (a * top1 - c * top0) * inverse
        table = table - left0 * new0 - left1 * new1
        return jnp.where(row == k, new0, jnp.where(row == k + 1, new1, table))

    table = lax.fori_loop(0, total // 2, step, table)
    scores_ref[...] = dot3(table, products, ((0,), (0,)))[total:total + docs]


def finish(stage, which, share, queries, pieces):
    n = len(pieces)
    docs, width = pieces[0].shape
    in_vmem = pl.BlockSpec(memory_space=pltpu.VMEM)
    return pl.pallas_call(
        functools.partial(final_kernel, n, share),
        out_shape=(
            jax.ShapeDtypeStruct((share, width), jnp.float32),
            jax.ShapeDtypeStruct((docs, queries.shape[0]), jnp.float32),
        ),
        in_specs=[pl.BlockSpec(memory_space=pltpu.SMEM)] + [in_vmem] * (n + 1),
        out_specs=(in_vmem, in_vmem),
        scratch_shapes=[pltpu.VMEM((n * docs, width), jnp.float32)],
        compiler_params=pltpu.CompilerParams(vmem_limit_bytes=32 * 1024 * 1024),
    )(jnp.stack([stage, which]).astype(jnp.int32), queries, *pieces)


def on_device(inputs, cotangent, gate_pre, down_weight, proj_in, proj_out, doc_lens, queries):
    n_groups, n_seq = lax.axis_size("groups"), lax.axis_size("seq")
    n_dp, n_tensor = lax.axis_size("dp"), lax.axis_size("tensor")
    group, half = lax.axis_index("groups"), lax.axis_index("seq")
    stage, side = lax.axis_index("dp"), lax.axis_index("tensor")
    rows = inputs.shape[0]
    units = gate_pre.shape[1]
    docs = doc_lens.shape[1]
    rank = proj_in.shape[1]
    width = rank * rank
    part = min(units, -(-units // (n_groups * n_seq * LANES)) * LANES)
    pair = ("groups", "seq")
    sizes = (n_groups, n_seq)
    mine = group * n_seq + half

    def first_unit(who):
        return jnp.minimum(who * part, units - part)

    start = first_unit(mine)

    lows = [low for low in CUTS if low < part]
    spans = list(zip(lows, lows[1:] + [part]))
    spans = spans[:1] + spans[3:] + spans[1:3]
    ring = [lax.dynamic_slice_in_dim(down_weight, start, part, 0)]

    def across(x, ds):
        return shifted(x, "seq", (n_seq,), (ds,))

    order = [(dg, ds) for dg in range(n_groups) for ds in range(n_seq)]

    def place(cot, dg, ds, r, block):
        at = ((side - r) % n_tensor) * block.shape[1]
        return lax.dynamic_update_slice(cot, block, ((dg * n_seq + ds) * rows, at))

    def unit_columns(dg, ds):
        to = ((group + dg) % n_groups) * n_seq + (half + ds) % n_seq
        return lax.dynamic_slice_in_dim(gate_pre, first_unit(to), part, 1)

    cots = {(0, 0, 0): cotangent}
    for dg in range(1, n_groups):
        cots[dg, 0, 0] = shifted(cotangent, "groups", (n_groups,), (dg,))
    for r in range(1, n_tensor):
        cots[0, 0, r] = shifted(cotangent, "tensor", (n_tensor,), (r,))
    sheets = {
        dg: jnp.concatenate([unit_columns(dg, ds) for ds in range(n_seq)], axis=0)
        for dg in range(n_groups)
    }
    beside = (0, 0, n_tensor - 1)
    sheets, cots[beside] = lax.optimization_barrier((sheets, cots[beside]))
    for dg in range(1, n_groups):
        sheets[dg] = shifted(sheets[dg], "groups", (n_groups,), (dg,))
    turned = shifted(ring[-1], "dp", (n_dp,), (1,))
    turned, cots = lax.optimization_barrier((turned, cots))
    ring.append(turned)

    gates, more = {}, {}

    def spread(dg, sheet):
        for ds in range(n_seq):
            x = sheet[ds * rows:(ds + 1) * rows]
            gates[dg, ds] = x if ds == 0 else across(x, ds)

    spread(0, sheets[0])
    for (dg, _, r), x in cots.items():
        for ds in range(1, n_seq):
            more[dg, ds, r] = across(x, ds)
    for dg in range(1, n_groups):
        for r in range(1, n_tensor):
            more[dg, 0, r] = shifted(cots[dg, 0, 0], "tensor", (n_tensor,), (r,))
    right_part = jnp.dot(inputs, proj_in, preferred_element_type=jnp.float32)
    out_factor = lax.dynamic_slice_in_dim(proj_out, start, part, 0)
    once = start + jnp.arange(part, dtype=jnp.int32) >= mine * part
    out_factor = jnp.where(once[:, None], out_factor, 0).astype(proj_out.dtype)
    factors = [out_factor[low:high] for low, high in spans]
    cot = jnp.zeros((len(order) * rows, n_tensor * cotangent.shape[1]), cotangent.dtype)
    for r in range(n_tensor):
        cot = place(cot, 0, 0, r, cots[0, 0, r])
    turned = shifted(ring[-1], "dp", (n_dp,), (1,)) if n_dp > 3 else ring.pop()
    turned, cot, cots, more, sheets, right_part, doc_lens, factors = lax.optimization_barrier(
        (turned, cot, cots, more, sheets, right_part, doc_lens, factors)
    )
    ring.append(turned)
    cots.update(more)

    while len(ring) < n_dp - 1:
        ring.append(shifted(ring[-1], "dp", (n_dp,), (1,)))
    cuts = [ring[-1][low:high] for low, high in spans]
    cuts, cot, cots, sheets, right_part, doc_lens = lax.optimization_barrier(
        (cuts, cot, cots, sheets, right_part, doc_lens)
    )
    turned = [shifted(cut, "dp", (n_dp,), (1,)) for cut in cuts]
    for dg in range(1, n_groups):
        for r in range(1, n_tensor):
            for ds in range(1, n_seq):
                cots[dg, ds, r] = across(cots[dg, 0, r], ds)
        spread(dg, sheets[dg])
    chunks = [ring + [block] for block in turned]
    right = sum_over(right_part, "tensor")
    rights = [right if dg == ds == 0 else shifted(right, pair, sizes, (dg, ds)) for dg, ds in order]
    lens = [doc_lens if dg == 0 else shifted(doc_lens, "groups", (n_groups,), (dg,)) for dg in range(n_groups)]

    gate = jnp.zeros((len(order) * rows, part), gate_pre.dtype)
    for (dg, ds, r), block in sorted(cots.items(), key=lambda item: (item[0][0] * item[0][2], item[0])):
        if (dg, ds) != (0, 0):
            cot = place(cot, dg, ds, r, block)
    for number, block in enumerate(order):
        gate = lax.dynamic_update_slice(gate, gates[block], (number * rows, 0))

    left = jnp.zeros((n_groups * n_seq * rows, rank), jnp.float32)
    me = jnp.reshape(stage, (1,)).astype(jnp.int32)
    for slots, (low, high), factor in zip(chunks, spans, factors):
        left = add_chunk(me, cot, gate, low, factor, left, slots, rows)

    parts = []
    for dg in range(n_groups):
        ends = jnp.cumsum(lens[dg][0])
        position = jnp.concatenate(
            [((half - ds) % n_seq) * rows + jnp.arange(rows, dtype=jnp.int32) for ds in range(n_seq)]
        )
        document = jnp.sum((position[:, None] >= ends[None, :]).astype(jnp.int32), axis=1)
        onehot = (document[:, None] == jnp.arange(docs, dtype=jnp.int32)[None, :]).astype(jnp.float32)
        span = slice(dg * n_seq * rows, (dg + 1) * n_seq * rows)
        right_block = jnp.concatenate(rights[dg * n_seq:(dg + 1) * n_seq], axis=0)
        grads = jnp.einsum(
            "tc,ti,tj->cij", onehot, left[span], right_block, precision=HIGHEST
        ).reshape(docs, width)
        parts.append(grads)
    grads = parts[0]
    for dg in range(1, n_groups):
        grads = grads + shifted(parts[dg], "groups", (n_groups,), (-dg,))
    doc_grads = sum_over(sum_over(grads, "tensor"), "seq")

    stages = [doc_grads if r == 0 else shifted(doc_grads, "dp", (n_dp,), (r,)) for r in range(n_dp)]
    share = width // (n_tensor * n_seq)
    fisher_rows, scores = finish(stage, side * n_seq + half, share, queries, stages)
    return (doc_grads, fisher_rows, scores.T)


def solution(mesh):
    return jax.shard_map(
        on_device,
        mesh=mesh,
        in_specs=(
            P(("groups", "dp", "seq"), "tensor"),
            P(("groups", "dp", "seq"), "tensor"),
            P(("groups", "dp", "seq"), "tensor"),
            P("tensor", "dp"),
            P("tensor", None),
            P("tensor", None),
            P(("groups", "dp"), None),
            P(),
        ),
        out_specs=(
            P(("groups", "dp"), None),
            P(("groups", "tensor", "seq"), None),
            P(None, ("groups", "dp")),
        ),
        check_vma=False,
    )
```

```python
import functools

import jax
import jax.numpy as jnp
from jax import lax
from jax.experimental import pallas as pl
from jax.experimental.pallas import tpu as pltpu
from jax.sharding import PartitionSpec as P

HIGHEST = lax.Precision.HIGHEST
CUTS = (0, 512, 768, 1024)
LANES = 128


def shifted(x, axes, sizes, shift):
    if isinstance(axes, str):
        (n,) = sizes
        pairs = [(i, (i + shift[0]) % n) for i in range(n)]
    else:
        a, b = sizes
        pairs = [
            (i * b + j, ((i + shift[0]) % a) * b + (j + shift[1]) % b)
            for i in range(a) for j in range(b)
        ]
    return lax.ppermute(x, axes, pairs)


def in_order(pieces, axis, dim):
    n = len(pieces)
    me = lax.axis_index(axis)
    shape = list(pieces[0].shape)
    size = shape[dim]
    shape[dim] *= n
    out = jnp.zeros(shape, pieces[0].dtype)
    for r, piece in enumerate(pieces):
        out = lax.dynamic_update_slice_in_dim(out, piece, ((me - r) % n) * size, dim)
    return out


def gather_in_order(x, axis, dim):
    n = lax.axis_size(axis)
    return in_order([x if r == 0 else shifted(x, axis, (n,), (r,)) for r in range(n)], axis, dim)


def sum_over(x, axis):
    n = lax.axis_size(axis)
    if n == 2:
        return x + shifted(x, axis, (2,), (1,))
    return jnp.sum(gather_in_order(x[None], axis, 0), axis=0)


def chunk_kernel(n, skip, me_ref, cot_ref, gate_ref, factor_ref, before_ref, *rest):
    slots, after_ref = rest[:n], rest[n]
    height, columns = slots[0].shape
    hidden = None
    for r in range(n):
        owner = lax.rem(me_ref[0] + (n - r), n)
        block = cot_ref[:, pl.ds(pl.multiple_of(owner * columns, columns), columns)]
        term = lax.dot_general(
            block, slots[r][...], (((1,), (1,)), ((), ())), preferred_element_type=jnp.float32
        )
        hidden = term if hidden is None else hidden + term
    gate = gate_ref[:, skip:skip + height].astype(jnp.float32)
    up_grad = (hidden * (gate / (1.0 + jnp.exp(-gate)))).astype(jnp.bfloat16)
    after_ref[...] = before_ref[...] + jnp.dot(
        up_grad, factor_ref[...], preferred_element_type=jnp.float32
    )


def add_chunk(me, cot, gate, low, factor, before, slots, tile):
    tokens, depth = cot.shape
    height, rank = factor.shape
    aligned = low % height == 0 and height % LANES == 0
    width, skip = (height, 0) if aligned else (gate.shape[1], low)
    at = low // height if aligned else 0
    n = len(slots)
    columns = slots[0].shape[1]
    if low % height:
        slots = [slot if slot.shape[0] == height else slot[low:low + height] for slot in slots]

    def weight_spec(slot):
        block = 0 if slot.shape[0] == height else low // height
        return pl.BlockSpec((height, columns), lambda i, me: (block, 0))

    return pl.pallas_call(
        functools.partial(chunk_kernel, n, skip),
        out_shape=jax.ShapeDtypeStruct((tokens, rank), jnp.float32),
        grid_spec=pltpu.PrefetchScalarGridSpec(
            num_scalar_prefetch=1,
            grid=(tokens // tile,),
            in_specs=[
                pl.BlockSpec((tile, depth), lambda i, me: (i, 0)),
                pl.BlockSpec((tile, width), lambda i, me: (i, at)),
                pl.BlockSpec((height, rank), lambda i, me: (0, 0)),
                pl.BlockSpec((tile, rank), lambda i, me: (i, 0)),
            ] + [weight_spec(slot) for slot in slots],
            out_specs=pl.BlockSpec((tile, rank), lambda i, me: (i, 0)),
        ),
        compiler_params=pltpu.CompilerParams(vmem_limit_bytes=36 * 1024 * 1024),
        cost_estimate=pl.CostEstimate(
            flops=2 * tokens * depth * height,
            bytes_accessed=2 * (tokens * depth + height * depth + tokens * height),
            transcendentals=tokens * height,
        ),
    )(me, cot, gate, factor, before, *slots)


def dot3(a, b, dims):
    a_high, b_high = a.astype(jnp.bfloat16), b.astype(jnp.bfloat16)
    a_low = (a - a_high.astype(jnp.float32)).astype(jnp.bfloat16)
    b_low = (b - b_high.astype(jnp.float32)).astype(jnp.bfloat16)
    dot = functools.partial(
        lax.dot_general, dimension_numbers=(dims, ((), ())), preferred_element_type=jnp.float32
    )
    return dot(a_high, b_high) + (dot(a_high, b_low) + dot(a_low, b_high))


def final_kernel(n, share, place_ref, queries_ref, *refs):
    pieces, (fisher_ref, scores_ref, every_ref) = refs[:n], refs[n:]
    docs, width = pieces[0].shape
    total = n * docs
    stage, which = place_ref[0], place_ref[1]
    for r in range(n):
        at = pl.multiple_of(lax.rem(stage + (n - r), n) * docs, docs)
        every_ref[pl.ds(at, docs), :] = pieces[r][...]
    every = every_ref[...]
    mean_diag = jnp.sum(jnp.sum(every * every, axis=1, keepdims=True), axis=0, keepdims=True) / width
    scale = 1.0 / mean_diag
    mine = every_ref[:, pl.ds(pl.multiple_of(which * share, share), share)]
    fisher_ref[...] = dot3(mine, every, ((0,), (0,))) * scale

    lanes = -(-(total + docs) // LANES) * LANES
    tall = jnp.concatenate([every, jnp.zeros((lanes - total, width), jnp.float32)], axis=0)
    row = lax.broadcasted_iota(jnp.int32, (total, lanes), 0)
    lane = lax.broadcasted_iota(jnp.int32, (total, lanes), 1)
    own = (lane >= total) & (lane - total == row - stage * docs) & (lane < total + docs)
    table = dot3(every, tall, ((1,), (1,))) * scale + jnp.where((lane == row) | own, 1.0, 0.0)
    products = dot3(every, queries_ref[...], ((1,), (1,)))

    def pick(condition, x, axis):
        return jnp.sum(jnp.where(condition, x, 0.0), axis=axis, keepdims=True)

    def step(i, table):
        k = 2 * i
        left0 = pick(lane == k, table, 1)
        left1 = pick(lane == k + 1, table, 1)
        top0 = pick(row == k, table, 0)
        top1 = pick(row == k + 1, table, 0)
        column = row[:, :1]
        a = pick(column == k, left0, 0)
        b = pick(column == k, left1, 0)
        c = pick(column == k + 1, left0, 0)
        d = pick(column == k + 1, left1, 0)
        inverse = 1.0 / (a * d - b * c)
        new0 = (d * top0 - b * top1) * inverse
        new1 = (a * top1 - c * top0) * inverse
        table = table - left0 * new0 - left1 * new1
        return jnp.where(row == k, new0, jnp.where(row == k + 1, new1, table))

    table = lax.fori_loop(0, total // 2, step, table)
    scores_ref[...] = dot3(table, products, ((0,), (0,)))[total:total + docs]


def finish(stage, which, share, queries, pieces):
    n = len(pieces)
    docs, width = pieces[0].shape
    in_vmem = pl.BlockSpec(memory_space=pltpu.VMEM)
    return pl.pallas_call(
        functools.partial(final_kernel, n, share),
        out_shape=(
            jax.ShapeDtypeStruct((share, width), jnp.float32),
            jax.ShapeDtypeStruct((docs, queries.shape[0]), jnp.float32),
        ),
        in_specs=[pl.BlockSpec(memory_space=pltpu.SMEM)] + [in_vmem] * (n + 1),
        out_specs=(in_vmem, in_vmem),
        scratch_shapes=[pltpu.VMEM((n * docs, width), jnp.float32)],
        compiler_params=pltpu.CompilerParams(vmem_limit_bytes=32 * 1024 * 1024),
    )(jnp.stack([stage, which]).astype(jnp.int32), queries, *pieces)


def on_device(inputs, cotangent, gate_pre, down_weight, proj_in, proj_out, doc_lens, queries):
    n_groups, n_seq = lax.axis_size("groups"), lax.axis_size("seq")
    n_dp, n_tensor = lax.axis_size("dp"), lax.axis_size("tensor")
    group, half = lax.axis_index("groups"), lax.axis_index("seq")
    stage, side = lax.axis_index("dp"), lax.axis_index("tensor")
    rows = inputs.shape[0]
    units = gate_pre.shape[1]
    docs = doc_lens.shape[1]
    rank = proj_in.shape[1]
    width = rank * rank
    part = min(units, -(-units // (n_groups * n_seq * LANES)) * LANES)
    pair = ("groups", "seq")
    sizes = (n_groups, n_seq)
    mine = group * n_seq + half

    def first_unit(who):
        return jnp.minimum(who * part, units - part)

    start = first_unit(mine)

    lows = [low for low in CUTS if low < part]
    spans = list(zip(lows, lows[1:] + [part]))
    spans = spans[:1] + spans[3:] + spans[1:3]
    ring = [lax.dynamic_slice_in_dim(down_weight, start, part, 0)]

    def across(x, ds):
        return shifted(x, "seq", (n_seq,), (ds,))

    order = [(dg, ds) for dg in range(n_groups) for ds in range(n_seq)]

    def place(cot, dg, ds, r, block):
        at = ((side - r) % n_tensor) * block.shape[1]
        return lax.dynamic_update_slice(cot, block, ((dg * n_seq + ds) * rows, at))

    def unit_columns(dg, ds):
        to = ((group + dg) % n_groups) * n_seq + (half + ds) % n_seq
        return lax.dynamic_slice_in_dim(gate_pre, first_unit(to), part, 1)

    cots = {(0, 0, 0): cotangent}
    for dg in range(1, n_groups):
        cots[dg, 0, 0] = shifted(cotangent, "groups", (n_groups,), (dg,))
    for r in range(1, n_tensor):
        cots[0, 0, r] = shifted(cotangent, "tensor", (n_tensor,), (r,))
    sheets = {
        dg: jnp.concatenate([unit_columns(dg, ds) for ds in range(n_seq)], axis=0)
        for dg in range(n_groups)
    }
    beside = (0, 0, n_tensor - 1)
    sheets, cots[beside] = lax.optimization_barrier((sheets, cots[beside]))
    for dg in range(1, n_groups):
        sheets[dg] = shifted(sheets[dg], "groups", (n_groups,), (dg,))
    turned = shifted(ring[-1], "dp", (n_dp,), (1,))
    right_part = jnp.dot(inputs, proj_in, preferred_element_type=jnp.float32)
    out_factor = lax.dynamic_slice_in_dim(proj_out, start, part, 0)
    once = start + jnp.arange(part, dtype=jnp.int32) >= mine * part
    out_factor = jnp.where(once[:, None], out_factor, 0).astype(proj_out.dtype)
    factors = [out_factor[low:high] for low, high in spans]
    turned, cots, right_part, factors = lax.optimization_barrier((turned, cots, right_part, factors))
    ring.append(turned)

    gates, more = {}, {}

    def spread(dg, sheet):
        for ds in range(n_seq):
            x = sheet[ds * rows:(ds + 1) * rows]
            gates[dg, ds] = x if ds == 0 else across(x, ds)

    spread(0, sheets[0])
    for (dg, _, r), x in cots.items():
        for ds in range(1, n_seq):
            more[dg, ds, r] = across(x, ds)
    for dg in range(1, n_groups):
        for r in range(1, n_tensor):
            more[dg, 0, r] = shifted(cots[dg, 0, 0], "tensor", (n_tensor,), (r,))
    cot = jnp.zeros((len(order) * rows, n_tensor * cotangent.shape[1]), cotangent.dtype)
    early = {**cots, **{key: block for key, block in more.items() if key[1] > 0}}
    for key, block in early.items():
        cot = place(cot, *key, block)
    turned = shifted(ring[-1], "dp", (n_dp,), (1,)) if n_dp > 3 else ring.pop()
    turned, cot, cots, more, sheets, right_part, doc_lens, factors = lax.optimization_barrier(
        (turned, cot, cots, more, sheets, right_part, doc_lens, factors)
    )
    ring.append(turned)
    cots.update(more)

    while len(ring) < n_dp - 1:
        ring.append(shifted(ring[-1], "dp", (n_dp,), (1,)))
    cuts = [ring[-1][low:high] for low, high in spans]
    cuts, cot, cots, sheets, right_part, doc_lens = lax.optimization_barrier(
        (cuts, cot, cots, sheets, right_part, doc_lens)
    )
    turned = [shifted(cut, "dp", (n_dp,), (1,)) for cut in cuts]
    for dg in range(1, n_groups):
        for r in range(1, n_tensor):
            for ds in range(1, n_seq):
                cots[dg, ds, r] = across(cots[dg, 0, r], ds)
        spread(dg, sheets[dg])
    chunks = [ring + [block] for block in turned]
    right = sum_over(right_part, "tensor")
    rights = [right if dg == ds == 0 else shifted(right, pair, sizes, (dg, ds)) for dg, ds in order]
    lens = [doc_lens if dg == 0 else shifted(doc_lens, "groups", (n_groups,), (dg,)) for dg in range(n_groups)]

    gate = jnp.zeros((len(order) * rows, part), gate_pre.dtype)
    for (dg, ds, r), block in sorted(cots.items(), key=lambda item: (item[0][0] * item[0][2], item[0])):
        if (dg, ds, r) not in early:
            cot = place(cot, dg, ds, r, block)
    for number, block in enumerate(order):
        gate = lax.dynamic_update_slice(gate, gates[block], (number * rows, 0))

    left = jnp.zeros((n_groups * n_seq * rows, rank), jnp.float32)
    me = jnp.reshape(stage, (1,)).astype(jnp.int32)
    for slots, (low, high), factor in zip(chunks, spans, factors):
        left = add_chunk(me, cot, gate, low, factor, left, slots, rows)

    parts = []
    for dg in range(n_groups):
        ends = jnp.cumsum(lens[dg][0])
        position = jnp.concatenate(
            [((half - ds) % n_seq) * rows + jnp.arange(rows, dtype=jnp.int32) for ds in range(n_seq)]
        )
        document = jnp.sum((position[:, None] >= ends[None, :]).astype(jnp.int32), axis=1)
        onehot = (document[:, None] == jnp.arange(docs, dtype=jnp.int32)[None, :]).astype(jnp.float32)
        span = slice(dg * n_seq * rows, (dg + 1) * n_seq * rows)
        right_block = jnp.concatenate(rights[dg * n_seq:(dg + 1) * n_seq], axis=0)
        grads = jnp.einsum(
            "tc,ti,tj->cij", onehot, left[span], right_block, precision=HIGHEST
        ).reshape(docs, width)
        parts.append(grads)
    grads = parts[0]
    for dg in range(1, n_groups):
        grads = grads + shifted(parts[dg], "groups", (n_groups,), (-dg,))
    doc_grads = sum_over(sum_over(grads, "tensor"), "seq")

    stages = [doc_grads if r == 0 else shifted(doc_grads, "dp", (n_dp,), (r,)) for r in range(n_dp)]
    share = width // (n_tensor * n_seq)
    fisher_rows, scores = finish(stage, side * n_seq + half, share, queries, stages)
    return (doc_grads, fisher_rows, scores.T)


def solution(mesh):
    return jax.shard_map(
        on_device,
        mesh=mesh,
        in_specs=(
            P(("groups", "dp", "seq"), "tensor"),
            P(("groups", "dp", "seq"), "tensor"),
            P(("groups", "dp", "seq"), "tensor"),
            P("tensor", "dp"),
            P("tensor", None),
            P("tensor", None),
            P(("groups", "dp"), None),
            P(),
        ),
        out_specs=(
            P(("groups", "dp"), None),
            P(("groups", "tensor", "seq"), None),
            P(None, ("groups", "dp")),
        ),
        check_vma=False,
    )
```

```python
import functools

import jax
import jax.numpy as jnp
from jax import lax
from jax.experimental import pallas as pl
from jax.experimental.pallas import tpu as pltpu
from jax.sharding import PartitionSpec as P

HIGHEST = lax.Precision.HIGHEST
CUTS = (0, 512, 768, 1024)
LANES = 128


def shifted(x, axes, sizes, shift):
    if isinstance(axes, str):
        (n,) = sizes
        pairs = [(i, (i + shift[0]) % n) for i in range(n)]
    else:
        a, b = sizes
        pairs = [
            (i * b + j, ((i + shift[0]) % a) * b + (j + shift[1]) % b)
            for i in range(a) for j in range(b)
        ]
    return lax.ppermute(x, axes, pairs)


def in_order(pieces, axis, dim):
    n = len(pieces)
    me = lax.axis_index(axis)
    shape = list(pieces[0].shape)
    size = shape[dim]
    shape[dim] *= n
    out = jnp.zeros(shape, pieces[0].dtype)
    for r, piece in enumerate(pieces):
        out = lax.dynamic_update_slice_in_dim(out, piece, ((me - r) % n) * size, dim)
    return out


def gather_in_order(x, axis, dim):
    n = lax.axis_size(axis)
    return in_order([x if r == 0 else shifted(x, axis, (n,), (r,)) for r in range(n)], axis, dim)


def sum_over(x, axis):
    n = lax.axis_size(axis)
    if n == 2:
        return x + shifted(x, axis, (2,), (1,))
    return jnp.sum(gather_in_order(x[None], axis, 0), axis=0)


def chunk_kernel(n, skip, me_ref, cot_ref, gate_ref, factor_ref, before_ref, *rest):
    slots, after_ref = rest[:n], rest[n]
    height, columns = slots[0].shape
    hidden = None
    for r in range(n):
        owner = lax.rem(me_ref[0] + (n - r), n)
        block = cot_ref[:, pl.ds(pl.multiple_of(owner * columns, columns), columns)]
        term = lax.dot_general(
            block, slots[r][...], (((1,), (1,)), ((), ())), preferred_element_type=jnp.float32
        )
        hidden = term if hidden is None else hidden + term
    gate = gate_ref[:, skip:skip + height].astype(jnp.float32)
    up_grad = (hidden * (gate / (1.0 + jnp.exp(-gate)))).astype(jnp.bfloat16)
    after_ref[...] = before_ref[...] + jnp.dot(
        up_grad, factor_ref[...], preferred_element_type=jnp.float32
    )


def add_chunk(me, cot, gate, low, factor, before, slots, tile):
    tokens, depth = cot.shape
    height, rank = factor.shape
    aligned = low % height == 0 and height % LANES == 0
    width, skip = (height, 0) if aligned else (gate.shape[1], low)
    at = low // height if aligned else 0
    n = len(slots)
    columns = slots[0].shape[1]
    if low % height:
        slots = [slot if slot.shape[0] == height else slot[low:low + height] for slot in slots]

    def weight_spec(slot):
        block = 0 if slot.shape[0] == height else low // height
        return pl.BlockSpec((height, columns), lambda i, me: (block, 0))

    return pl.pallas_call(
        functools.partial(chunk_kernel, n, skip),
        out_shape=jax.ShapeDtypeStruct((tokens, rank), jnp.float32),
        grid_spec=pltpu.PrefetchScalarGridSpec(
            num_scalar_prefetch=1,
            grid=(tokens // tile,),
            in_specs=[
                pl.BlockSpec((tile, depth), lambda i, me: (i, 0)),
                pl.BlockSpec((tile, width), lambda i, me: (i, at)),
                pl.BlockSpec((height, rank), lambda i, me: (0, 0)),
                pl.BlockSpec((tile, rank), lambda i, me: (i, 0)),
            ] + [weight_spec(slot) for slot in slots],
            out_specs=pl.BlockSpec((tile, rank), lambda i, me: (i, 0)),
        ),
        compiler_params=pltpu.CompilerParams(vmem_limit_bytes=36 * 1024 * 1024),
        cost_estimate=pl.CostEstimate(
            flops=2 * tokens * depth * height,
            bytes_accessed=2 * (tokens * depth + height * depth + tokens * height),
            transcendentals=tokens * height,
        ),
    )(me, cot, gate, factor, before, *slots)


def dot3(a, b, dims):
    a_high, b_high = a.astype(jnp.bfloat16), b.astype(jnp.bfloat16)
    a_low = (a - a_high.astype(jnp.float32)).astype(jnp.bfloat16)
    b_low = (b - b_high.astype(jnp.float32)).astype(jnp.bfloat16)
    dot = functools.partial(
        lax.dot_general, dimension_numbers=(dims, ((), ())), preferred_element_type=jnp.float32
    )
    return dot(a_high, b_high) + (dot(a_high, b_low) + dot(a_low, b_high))


def final_kernel(n, share, place_ref, queries_ref, *refs):
    pieces, (fisher_ref, scores_ref, every_ref) = refs[:n], refs[n:]
    docs, width = pieces[0].shape
    total = n * docs
    stage, which = place_ref[0], place_ref[1]
    for r in range(n):
        at = pl.multiple_of(lax.rem(stage + (n - r), n) * docs, docs)
        every_ref[pl.ds(at, docs), :] = pieces[r][...]
    every = every_ref[...]
    mean_diag = jnp.sum(jnp.sum(every * every, axis=1, keepdims=True), axis=0, keepdims=True) / width
    scale = 1.0 / mean_diag
    mine = every_ref[:, pl.ds(pl.multiple_of(which * share, share), share)]
    fisher_ref[...] = dot3(mine, every, ((0,), (0,))) * scale

    lanes = -(-(total + docs) // LANES) * LANES
    tall = jnp.concatenate([every, jnp.zeros((lanes - total, width), jnp.float32)], axis=0)
    row = lax.broadcasted_iota(jnp.int32, (total, lanes), 0)
    lane = lax.broadcasted_iota(jnp.int32, (total, lanes), 1)
    own = (lane >= total) & (lane - total == row - stage * docs) & (lane < total + docs)
    table = dot3(every, tall, ((1,), (1,))) * scale + jnp.where((lane == row) | own, 1.0, 0.0)
    products = dot3(every, queries_ref[...], ((1,), (1,)))

    def pick(condition, x, axis):
        return jnp.sum(jnp.where(condition, x, 0.0), axis=axis, keepdims=True)

    def step(i, table):
        k = 2 * i
        left0 = pick(lane == k, table, 1)
        left1 = pick(lane == k + 1, table, 1)
        top0 = pick(row == k, table, 0)
        top1 = pick(row == k + 1, table, 0)
        column = row[:, :1]
        a = pick(column == k, left0, 0)
        b = pick(column == k, left1, 0)
        c = pick(column == k + 1, left0, 0)
        d = pick(column == k + 1, left1, 0)
        inverse = 1.0 / (a * d - b * c)
        new0 = (d * top0 - b * top1) * inverse
        new1 = (a * top1 - c * top0) * inverse
        table = table - left0 * new0 - left1 * new1
        return jnp.where(row == k, new0, jnp.where(row == k + 1, new1, table))

    table = lax.fori_loop(0, total // 2, step, table)
    scores_ref[...] = dot3(table, products, ((0,), (0,)))[total:total + docs]


def finish(stage, which, share, queries, pieces):
    n = len(pieces)
    docs, width = pieces[0].shape
    in_vmem = pl.BlockSpec(memory_space=pltpu.VMEM)
    return pl.pallas_call(
        functools.partial(final_kernel, n, share),
        out_shape=(
            jax.ShapeDtypeStruct((share, width), jnp.float32),
            jax.ShapeDtypeStruct((docs, queries.shape[0]), jnp.float32),
        ),
        in_specs=[pl.BlockSpec(memory_space=pltpu.SMEM)] + [in_vmem] * (n + 1),
        out_specs=(in_vmem, in_vmem),
        scratch_shapes=[pltpu.VMEM((n * docs, width), jnp.float32)],
        compiler_params=pltpu.CompilerParams(vmem_limit_bytes=32 * 1024 * 1024),
    )(jnp.stack([stage, which]).astype(jnp.int32), queries, *pieces)


def on_device(inputs, cotangent, gate_pre, down_weight, proj_in, proj_out, doc_lens, queries):
    n_groups, n_seq = lax.axis_size("groups"), lax.axis_size("seq")
    n_dp, n_tensor = lax.axis_size("dp"), lax.axis_size("tensor")
    group, half = lax.axis_index("groups"), lax.axis_index("seq")
    stage, side = lax.axis_index("dp"), lax.axis_index("tensor")
    rows = inputs.shape[0]
    units = gate_pre.shape[1]
    docs = doc_lens.shape[1]
    rank = proj_in.shape[1]
    width = rank * rank
    part = min(units, -(-units // (n_groups * n_seq * LANES)) * LANES)
    pair = ("groups", "seq")
    sizes = (n_groups, n_seq)
    mine = group * n_seq + half

    def first_unit(who):
        return jnp.minimum(who * part, units - part)

    start = first_unit(mine)

    lows = [low for low in CUTS if low < part]
    spans = list(zip(lows, lows[1:] + [part]))
    spans = spans[:1] + spans[3:] + spans[1:3]
    ring = [lax.dynamic_slice_in_dim(down_weight, start, part, 0)]

    def across(x, ds):
        return shifted(x, "seq", (n_seq,), (ds,))

    order = [(dg, ds) for dg in range(n_groups) for ds in range(n_seq)]

    def place(cot, dg, ds, r, block):
        at = ((side - r) % n_tensor) * block.shape[1]
        return lax.dynamic_update_slice(cot, block, ((dg * n_seq + ds) * rows, at))

    def unit_columns(dg, ds):
        to = ((group + dg) % n_groups) * n_seq + (half + ds) % n_seq
        return lax.dynamic_slice_in_dim(gate_pre, first_unit(to), part, 1)

    cots = {(0, 0, 0): cotangent}
    for dg in range(1, n_groups):
        cots[dg, 0, 0] = shifted(cotangent, "groups", (n_groups,), (dg,))
    for r in range(1, n_tensor):
        cots[0, 0, r] = shifted(cotangent, "tensor", (n_tensor,), (r,))
    sheets = {
        dg: jnp.concatenate([unit_columns(dg, ds) for ds in range(n_seq)], axis=0)
        for dg in range(n_groups)
    }
    beside = (0, 0, n_tensor - 1)
    sheets, cots[beside] = lax.optimization_barrier((sheets, cots[beside]))
    for dg in range(1, n_groups):
        sheets[dg] = shifted(sheets[dg], "groups", (n_groups,), (dg,))
    turned = shifted(ring[-1], "dp", (n_dp,), (1,))
    right_part = jnp.dot(inputs, proj_in, preferred_element_type=jnp.float32)
    out_factor = lax.dynamic_slice_in_dim(proj_out, start, part, 0)
    once = start + jnp.arange(part, dtype=jnp.int32) >= mine * part
    out_factor = jnp.where(once[:, None], out_factor, 0).astype(proj_out.dtype)
    factors = [out_factor[low:high] for low, high in spans]
    turned, cots, right_part, factors = lax.optimization_barrier((turned, cots, right_part, factors))
    ring.append(turned)

    gates, more = {}, {}

    def spread(dg, sheet):
        for ds in range(n_seq):
            x = sheet[ds * rows:(ds + 1) * rows]
            gates[dg, ds] = x if ds == 0 else across(x, ds)

    spread(0, sheets[0])
    for (dg, _, r), x in cots.items():
        for ds in range(1, n_seq):
            more[dg, ds, r] = across(x, ds)
    for dg in range(1, n_groups):
        for r in range(1, n_tensor):
            more[dg, 0, r] = shifted(cots[dg, 0, 0], "tensor", (n_tensor,), (r,))
    cot = jnp.zeros((len(order) * rows, n_tensor * cotangent.shape[1]), cotangent.dtype)
    early = {**cots, **{key: block for key, block in more.items() if key[1] > 0}}
    for key, block in early.items():
        cot = place(cot, *key, block)
    turned = shifted(ring[-1], "dp", (n_dp,), (1,)) if n_dp > 3 else ring.pop()
    uneven = [c for c, (low, high) in enumerate(spans) if low % (high - low)]
    kept = {c: [slot[slice(*spans[c])] for slot in ring[:2]] for c in uneven}
    turned, cot, cots, more, sheets, right_part, doc_lens, factors, kept = lax.optimization_barrier(
        (turned, cot, cots, more, sheets, right_part, doc_lens, factors, kept)
    )
    ring.append(turned)
    cots.update(more)

    while len(ring) < n_dp - 1:
        ring.append(shifted(ring[-1], "dp", (n_dp,), (1,)))
    cuts = [ring[-1][low:high] for low, high in spans]
    cuts, cot, cots, sheets, right_part, doc_lens = lax.optimization_barrier(
        (cuts, cot, cots, sheets, right_part, doc_lens)
    )
    turned = [shifted(cut, "dp", (n_dp,), (1,)) for cut in cuts]
    for dg in range(1, n_groups):
        for r in range(1, n_tensor):
            for ds in range(1, n_seq):
                cots[dg, ds, r] = across(cots[dg, 0, r], ds)
        spread(dg, sheets[dg])
    chunks = [
        (kept[c] + [slot[slice(*spans[c])] for slot in ring[2:-1]] + [cuts[c]] if c in kept else ring) + [block]
        for c, block in enumerate(turned)
    ]
    beside = (n_groups - 1, n_seq - 1)
    right_part, doc_lens, gates[beside] = lax.optimization_barrier((right_part, doc_lens, gates[beside]))
    right = sum_over(right_part, "tensor")
    rights = [right if dg == ds == 0 else shifted(right, pair, sizes, (dg, ds)) for dg, ds in order]
    lens = [doc_lens if dg == 0 else shifted(doc_lens, "groups", (n_groups,), (dg,)) for dg in range(n_groups)]

    gate = jnp.zeros((len(order) * rows, part), gate_pre.dtype)
    for (dg, ds, r), block in sorted(cots.items(), key=lambda item: (item[0][0] * item[0][2], item[0])):
        if (dg, ds, r) not in early:
            cot = place(cot, dg, ds, r, block)
    for number, block in enumerate(order):
        gate = lax.dynamic_update_slice(gate, gates[block], (number * rows, 0))

    left = jnp.zeros((n_groups * n_seq * rows, rank), jnp.float32)
    me = jnp.reshape(stage, (1,)).astype(jnp.int32)
    for slots, (low, high), factor in zip(chunks, spans, factors):
        left = add_chunk(me, cot, gate, low, factor, left, slots, rows)

    parts = []
    for dg in range(n_groups):
        ends = jnp.cumsum(lens[dg][0])
        position = jnp.concatenate(
            [((half - ds) % n_seq) * rows + jnp.arange(rows, dtype=jnp.int32) for ds in range(n_seq)]
        )
        document = jnp.sum((position[:, None] >= ends[None, :]).astype(jnp.int32), axis=1)
        onehot = (document[:, None] == jnp.arange(docs, dtype=jnp.int32)[None, :]).astype(jnp.float32)
        span = slice(dg * n_seq * rows, (dg + 1) * n_seq * rows)
        right_block = jnp.concatenate(rights[dg * n_seq:(dg + 1) * n_seq], axis=0)
        grads = jnp.einsum(
            "tc,ti,tj->cij", onehot, left[span], right_block, precision=HIGHEST
        ).reshape(docs, width)
        parts.append(grads)
    grads = parts[0]
    for dg in range(1, n_groups):
        grads = grads + shifted(parts[dg], "groups", (n_groups,), (-dg,))
    doc_grads = sum_over(sum_over(grads, "tensor"), "seq")

    stages = [doc_grads if r == 0 else shifted(doc_grads, "dp", (n_dp,), (r,)) for r in range(n_dp)]
    share = width // (n_tensor * n_seq)
    fisher_rows, scores = finish(stage, side * n_seq + half, share, queries, stages)
    return (doc_grads, fisher_rows, scores.T)


def solution(mesh):
    return jax.shard_map(
        on_device,
        mesh=mesh,
        in_specs=(
            P(("groups", "dp", "seq"), "tensor"),
            P(("groups", "dp", "seq"), "tensor"),
            P(("groups", "dp", "seq"), "tensor"),
            P("tensor", "dp"),
            P("tensor", None),
            P("tensor", None),
            P(("groups", "dp"), None),
            P(),
        ),
        out_specs=(
            P(("groups", "dp"), None),
            P(("groups", "tensor", "seq"), None),
            P(None, ("groups", "dp")),
        ),
        check_vma=False,
    )
```

```python
import functools

import jax
import jax.numpy as jnp
from jax import lax
from jax.experimental import pallas as pl
from jax.experimental.pallas import tpu as pltpu
from jax.sharding import PartitionSpec as P

HIGHEST = lax.Precision.HIGHEST
CUTS = (0, 512, 768, 1024)
LANES = 128


def shifted(x, axes, sizes, shift):
    if isinstance(axes, str):
        (n,) = sizes
        pairs = [(i, (i + shift[0]) % n) for i in range(n)]
    else:
        a, b = sizes
        pairs = [
            (i * b + j, ((i + shift[0]) % a) * b + (j + shift[1]) % b)
            for i in range(a) for j in range(b)
        ]
    return lax.ppermute(x, axes, pairs)


def in_order(pieces, axis, dim):
    n = len(pieces)
    me = lax.axis_index(axis)
    shape = list(pieces[0].shape)
    size = shape[dim]
    shape[dim] *= n
    out = jnp.zeros(shape, pieces[0].dtype)
    for r, piece in enumerate(pieces):
        out = lax.dynamic_update_slice_in_dim(out, piece, ((me - r) % n) * size, dim)
    return out


def gather_in_order(x, axis, dim):
    n = lax.axis_size(axis)
    return in_order([x if r == 0 else shifted(x, axis, (n,), (r,)) for r in range(n)], axis, dim)


def sum_over(x, axis):
    n = lax.axis_size(axis)
    if n == 2:
        return x + shifted(x, axis, (2,), (1,))
    return jnp.sum(gather_in_order(x[None], axis, 0), axis=0)


def chunk_kernel(n, skip, me_ref, cot_ref, gate_ref, factor_ref, before_ref, *rest):
    slots, after_ref = rest[:n], rest[n]
    height, columns = slots[0].shape
    hidden = None
    for r in range(n):
        owner = lax.rem(me_ref[0] + (n - r), n)
        block = cot_ref[:, pl.ds(pl.multiple_of(owner * columns, columns), columns)]
        term = lax.dot_general(
            block, slots[r][...], (((1,), (1,)), ((), ())), preferred_element_type=jnp.float32
        )
        hidden = term if hidden is None else hidden + term
    gate = gate_ref[:, skip:skip + height].astype(jnp.float32)
    up_grad = (hidden * (gate / (1.0 + jnp.exp(-gate)))).astype(jnp.bfloat16)
    after_ref[...] = before_ref[...] + jnp.dot(
        up_grad, factor_ref[...], preferred_element_type=jnp.float32
    )


def add_chunk(me, cot, gate, low, factor, before, slots, tile):
    tokens, depth = cot.shape
    height, rank = factor.shape
    aligned = low % height == 0 and height % LANES == 0
    width, skip = (height, 0) if aligned else (gate.shape[1], low)
    at = low // height if aligned else 0
    n = len(slots)
    columns = slots[0].shape[1]
    if low % height:
        slots = [slot if slot.shape[0] == height else slot[low:low + height] for slot in slots]

    def weight_spec(slot):
        block = 0 if slot.shape[0] == height else low // height
        return pl.BlockSpec((height, columns), lambda i, me: (block, 0))

    return pl.pallas_call(
        functools.partial(chunk_kernel, n, skip),
        out_shape=jax.ShapeDtypeStruct((tokens, rank), jnp.float32),
        grid_spec=pltpu.PrefetchScalarGridSpec(
            num_scalar_prefetch=1,
            grid=(tokens // tile,),
            in_specs=[
                pl.BlockSpec((tile, depth), lambda i, me: (i, 0)),
                pl.BlockSpec((tile, width), lambda i, me: (i, at)),
                pl.BlockSpec((height, rank), lambda i, me: (0, 0)),
                pl.BlockSpec((tile, rank), lambda i, me: (i, 0)),
            ] + [weight_spec(slot) for slot in slots],
            out_specs=pl.BlockSpec((tile, rank), lambda i, me: (i, 0)),
        ),
        compiler_params=pltpu.CompilerParams(vmem_limit_bytes=36 * 1024 * 1024),
        cost_estimate=pl.CostEstimate(
            flops=2 * tokens * depth * height,
            bytes_accessed=2 * (tokens * depth + height * depth + tokens * height),
            transcendentals=tokens * height,
        ),
    )(me, cot, gate, factor, before, *slots)


def dot3(a, b, dims):
    a_high, b_high = a.astype(jnp.bfloat16), b.astype(jnp.bfloat16)
    a_low = (a - a_high.astype(jnp.float32)).astype(jnp.bfloat16)
    b_low = (b - b_high.astype(jnp.float32)).astype(jnp.bfloat16)
    dot = functools.partial(
        lax.dot_general, dimension_numbers=(dims, ((), ())), preferred_element_type=jnp.float32
    )
    return dot(a_high, b_high) + (dot(a_high, b_low) + dot(a_low, b_high))


def final_kernel(n, share, place_ref, queries_ref, *refs):
    pieces, (fisher_ref, scores_ref, every_ref, held_ref, sem) = refs[:n], refs[n:]
    copy = pltpu.make_async_copy(queries_ref, held_ref, sem)
    copy.start()
    docs, width = pieces[0].shape
    total = n * docs
    stage, which = place_ref[0], place_ref[1]
    for r in range(n):
        at = pl.multiple_of(lax.rem(stage + (n - r), n) * docs, docs)
        every_ref[pl.ds(at, docs), :] = pieces[r][...]
    every = every_ref[...]
    mean_diag = jnp.sum(jnp.sum(every * every, axis=1, keepdims=True), axis=0, keepdims=True) / width
    scale = 1.0 / mean_diag
    mine = every_ref[:, pl.ds(pl.multiple_of(which * share, share), share)]
    fisher_ref[...] = dot3(mine, every, ((0,), (0,))) * scale

    lanes = -(-(total + docs) // LANES) * LANES
    tall = jnp.concatenate([every, jnp.zeros((lanes - total, width), jnp.float32)], axis=0)
    row = lax.broadcasted_iota(jnp.int32, (total, lanes), 0)
    lane = lax.broadcasted_iota(jnp.int32, (total, lanes), 1)
    own = (lane >= total) & (lane - total == row - stage * docs) & (lane < total + docs)
    table = dot3(every, tall, ((1,), (1,))) * scale + jnp.where((lane == row) | own, 1.0, 0.0)

    def pick(condition, x, axis):
        return jnp.sum(jnp.where(condition, x, 0.0), axis=axis, keepdims=True)

    def step(i, table):
        k = 2 * i
        left0 = pick(lane == k, table, 1)
        left1 = pick(lane == k + 1, table, 1)
        top0 = pick(row == k, table, 0)
        top1 = pick(row == k + 1, table, 0)
        column = row[:, :1]
        a = pick(column == k, left0, 0)
        b = pick(column == k, left1, 0)
        c = pick(column == k + 1, left0, 0)
        d = pick(column == k + 1, left1, 0)
        inverse = 1.0 / (a * d - b * c)
        new0 = (d * top0 - b * top1) * inverse
        new1 = (a * top1 - c * top0) * inverse
        table = table - left0 * new0 - left1 * new1
        return jnp.where(row == k, new0, jnp.where(row == k + 1, new1, table))

    table = lax.fori_loop(0, total // 2, step, table)
    copy.wait()
    products = dot3(every, held_ref[...], ((1,), (1,)))
    scores_ref[...] = dot3(table, products, ((0,), (0,)))[total:total + docs]


def finish(stage, which, share, queries, pieces):
    n = len(pieces)
    docs, width = pieces[0].shape
    in_vmem = pl.BlockSpec(memory_space=pltpu.VMEM)
    return pl.pallas_call(
        functools.partial(final_kernel, n, share),
        out_shape=(
            jax.ShapeDtypeStruct((share, width), jnp.float32),
            jax.ShapeDtypeStruct((docs, queries.shape[0]), jnp.float32),
        ),
        in_specs=[pl.BlockSpec(memory_space=pltpu.SMEM), pl.BlockSpec(memory_space=pl.ANY)] + [in_vmem] * n,
        out_specs=(in_vmem, in_vmem),
        scratch_shapes=[
            pltpu.VMEM((n * docs, width), jnp.float32),
            pltpu.VMEM(queries.shape, jnp.float32),
            pltpu.SemaphoreType.DMA,
        ],
        compiler_params=pltpu.CompilerParams(vmem_limit_bytes=56 * 1024 * 1024),
    )(jnp.stack([stage, which]).astype(jnp.int32), queries, *pieces)


def on_device(inputs, cotangent, gate_pre, down_weight, proj_in, proj_out, doc_lens, queries):
    n_groups, n_seq = lax.axis_size("groups"), lax.axis_size("seq")
    n_dp, n_tensor = lax.axis_size("dp"), lax.axis_size("tensor")
    group, half = lax.axis_index("groups"), lax.axis_index("seq")
    stage, side = lax.axis_index("dp"), lax.axis_index("tensor")
    rows = inputs.shape[0]
    units = gate_pre.shape[1]
    docs = doc_lens.shape[1]
    rank = proj_in.shape[1]
    width = rank * rank
    part = min(units, -(-units // (n_groups * n_seq * LANES)) * LANES)
    pair = ("groups", "seq")
    sizes = (n_groups, n_seq)
    mine = group * n_seq + half

    def first_unit(who):
        return jnp.minimum(who * part, units - part)

    start = first_unit(mine)

    lows = [low for low in CUTS if low < part]
    spans = list(zip(lows, lows[1:] + [part]))
    spans = spans[:1] + spans[3:] + spans[1:3]
    ring = [lax.dynamic_slice_in_dim(down_weight, start, part, 0)]

    def across(x, ds):
        return shifted(x, "seq", (n_seq,), (ds,))

    order = [(dg, ds) for dg in range(n_groups) for ds in range(n_seq)]

    def place(cot, dg, ds, r, block):
        at = ((side - r) % n_tensor) * block.shape[1]
        return lax.dynamic_update_slice(cot, block, ((dg * n_seq + ds) * rows, at))

    def unit_columns(dg, ds):
        to = ((group + dg) % n_groups) * n_seq + (half + ds) % n_seq
        return lax.dynamic_slice_in_dim(gate_pre, first_unit(to), part, 1)

    cots = {(0, 0, 0): cotangent}
    for dg in range(1, n_groups):
        cots[dg, 0, 0] = shifted(cotangent, "groups", (n_groups,), (dg,))
    for r in range(1, n_tensor):
        cots[0, 0, r] = shifted(cotangent, "tensor", (n_tensor,), (r,))
    sheets = {
        dg: jnp.concatenate([unit_columns(dg, ds) for ds in range(n_seq)], axis=0)
        for dg in range(n_groups)
    }
    beside = (0, 0, n_tensor - 1)
    sheets, cots[beside] = lax.optimization_barrier((sheets, cots[beside]))
    for dg in range(1, n_groups):
        sheets[dg] = shifted(sheets[dg], "groups", (n_groups,), (dg,))
    turned = shifted(ring[-1], "dp", (n_dp,), (1,))
    right_part = jnp.dot(inputs, proj_in, preferred_element_type=jnp.float32)
    out_factor = lax.dynamic_slice_in_dim(proj_out, start, part, 0)
    once = start + jnp.arange(part, dtype=jnp.int32) >= mine * part
    out_factor = jnp.where(once[:, None], out_factor, 0).astype(proj_out.dtype)
    factors = [out_factor[low:high] for low, high in spans]
    turned, cots, right_part, factors = lax.optimization_barrier((turned, cots, right_part, factors))
    ring.append(turned)

    gates, more = {}, {}

    def spread(dg, sheet):
        for ds in range(n_seq):
            x = sheet[ds * rows:(ds + 1) * rows]
            gates[dg, ds] = x if ds == 0 else across(x, ds)

    spread(0, sheets[0])
    for (dg, _, r), x in cots.items():
        for ds in range(1, n_seq):
            more[dg, ds, r] = across(x, ds)
    for dg in range(1, n_groups):
        for r in range(1, n_tensor):
            more[dg, 0, r] = shifted(cots[dg, 0, 0], "tensor", (n_tensor,), (r,))
    cot = jnp.zeros((len(order) * rows, n_tensor * cotangent.shape[1]), cotangent.dtype)
    early = {**cots, **{key: block for key, block in more.items() if key[1] > 0}}
    for key, block in early.items():
        cot = place(cot, *key, block)
    turned = shifted(ring[-1], "dp", (n_dp,), (1,)) if n_dp > 3 else ring.pop()
    uneven = [c for c, (low, high) in enumerate(spans) if low % (high - low)]
    kept = {c: [slot[slice(*spans[c])] for slot in ring[:2]] for c in uneven}
    turned, cot, cots, more, sheets, right_part, doc_lens, factors, kept = lax.optimization_barrier(
        (turned, cot, cots, more, sheets, right_part, doc_lens, factors, kept)
    )
    ring.append(turned)
    cots.update(more)

    while len(ring) < n_dp - 1:
        ring.append(shifted(ring[-1], "dp", (n_dp,), (1,)))
    cuts = [ring[-1][low:high] for low, high in spans]
    cuts, cot, cots, sheets, right_part, doc_lens = lax.optimization_barrier(
        (cuts, cot, cots, sheets, right_part, doc_lens)
    )
    turned = [shifted(cut, "dp", (n_dp,), (1,)) for cut in cuts]
    for dg in range(1, n_groups):
        for r in range(1, n_tensor):
            for ds in range(1, n_seq):
                cots[dg, ds, r] = across(cots[dg, 0, r], ds)
        spread(dg, sheets[dg])
    chunks = [
        (kept[c] + [slot[slice(*spans[c])] for slot in ring[2:-1]] + [cuts[c]] if c in kept else ring) + [block]
        for c, block in enumerate(turned)
    ]
    beside = (n_groups - 1, n_seq - 1)
    right_part, doc_lens, gates[beside] = lax.optimization_barrier((right_part, doc_lens, gates[beside]))
    right = sum_over(right_part, "tensor")
    rights = [right if dg == ds == 0 else shifted(right, pair, sizes, (dg, ds)) for dg, ds in order]
    lens = [doc_lens if dg == 0 else shifted(doc_lens, "groups", (n_groups,), (dg,)) for dg in range(n_groups)]

    gate = jnp.zeros((len(order) * rows, part), gate_pre.dtype)
    for (dg, ds, r), block in sorted(cots.items(), key=lambda item: (item[0][0] * item[0][2], item[0])):
        if (dg, ds, r) not in early:
            cot = place(cot, dg, ds, r, block)
    for number, block in enumerate(order):
        gate = lax.dynamic_update_slice(gate, gates[block], (number * rows, 0))

    left = jnp.zeros((n_groups * n_seq * rows, rank), jnp.float32)
    me = jnp.reshape(stage, (1,)).astype(jnp.int32)
    for slots, (low, high), factor in zip(chunks, spans, factors):
        left = add_chunk(me, cot, gate, low, factor, left, slots, rows)

    parts = []
    for dg in range(n_groups):
        ends = jnp.cumsum(lens[dg][0])
        position = jnp.concatenate(
            [((half - ds) % n_seq) * rows + jnp.arange(rows, dtype=jnp.int32) for ds in range(n_seq)]
        )
        document = jnp.sum((position[:, None] >= ends[None, :]).astype(jnp.int32), axis=1)
        onehot = (document[:, None] == jnp.arange(docs, dtype=jnp.int32)[None, :]).astype(jnp.float32)
        span = slice(dg * n_seq * rows, (dg + 1) * n_seq * rows)
        right_block = jnp.concatenate(rights[dg * n_seq:(dg + 1) * n_seq], axis=0)
        grads = jnp.einsum(
            "tc,ti,tj->cij", onehot, left[span], right_block, precision=HIGHEST
        ).reshape(docs, width)
        parts.append(grads)
    grads = parts[0]
    for dg in range(1, n_groups):
        grads = grads + shifted(parts[dg], "groups", (n_groups,), (-dg,))
    doc_grads = sum_over(sum_over(grads, "tensor"), "seq")

    stages = [doc_grads if r == 0 else shifted(doc_grads, "dp", (n_dp,), (r,)) for r in range(n_dp)]
    share = width // (n_tensor * n_seq)
    fisher_rows, scores = finish(stage, side * n_seq + half, share, queries, stages)
    return (doc_grads, fisher_rows, scores.T)


def solution(mesh):
    return jax.shard_map(
        on_device,
        mesh=mesh,
        in_specs=(
            P(("groups", "dp", "seq"), "tensor"),
            P(("groups", "dp", "seq"), "tensor"),
            P(("groups", "dp", "seq"), "tensor"),
            P("tensor", "dp"),
            P("tensor", None),
            P("tensor", None),
            P(("groups", "dp"), None),
            P(),
        ),
        out_specs=(
            P(("groups", "dp"), None),
            P(("groups", "tensor", "seq"), None),
            P(None, ("groups", "dp")),
        ),
        check_vma=False,
    )
```
